256 devices in a mesh: clip: 4 (over z_lo), seg: 64 (over x, y, z_hi, core).
Axes of the slice: x: 4, y: 4, z: 8 (z_hi: 2, z_lo: 4; z = z_hi * 4 + z_lo), core: 2. Of those that a mesh axis runs over, the one named last changes fastest.
Arguments:
- spectra: bfloat16 [16, 2, 1024, 1536], P('clip', None, 'seg'), may hold values from -6 to 6
- target: bfloat16 [16, 786432], P('clip', 'seg'), may hold values from -12 to 12
- lengths: int32 [16], P('clip'), may hold values from 768 to 1536, as said below
Outputs:
- loss: float32 [], replicated
- spec_grad: bfloat16 [16, 2, 1024, 1536], P('clip', None, 'seg')
The draws below stay inside these ranges and needn't reach their ends.
Inputs may be any that keep to these rules, and one draw needn't show every extreme that they name: `lengths`: some clip has all 1536 frames.
All inputs are finite; a program needn't handle non-finite values.
Results may differ from the reference program's by a relative error of at most 0.0092.
Values may be sent and summed in bfloat16 or wider, within the bound.
A program may use at most 128 MiB of HBM per device.

```python
import math
import jax
import jax.numpy as jnp
from jax import lax

BINS = 1024
NFFT = 2048
HOP = 512
CLIPS = 16
FRAMES = 1536
SAMPLES = 786432


def draw_target(key, part):
    gaussian = jax.random.normal(jax.random.fold_in(key, 11), (CLIPS, SAMPLES), jnp.float32)
    position = jnp.arange(SAMPLES).astype(jnp.float32) / SAMPLES
    signal = gaussian * jnp.sqrt(1.0 + 2.0 * position)[None, :]
    return jnp.clip(signal, -12.0, 12.0).astype(jnp.bfloat16)


def draw_lengths(key, part):
    drawn = jax.random.randint(jax.random.fold_in(key, 21), (CLIPS,), FRAMES // 2, FRAMES + 1)
    longest = jax.random.randint(jax.random.fold_in(key, 22), (), 0, CLIPS)
    return jnp.where(jnp.arange(CLIPS) == longest, FRAMES, drawn).astype(jnp.int32)


def block_scale(rng, extent, shards, least, top_value):
    gain = 1.0
    for axis_at, parts in shards:
        draws = jax.random.uniform(jax.random.fold_in(jax.random.fold_in(rng, 6), axis_at), (parts,), jnp.float32, least / len(shards), top_value / len(shards))
        gain = gain * jnp.repeat(jnp.exp(draws), extent[axis_at] // parts).reshape((-1,) + (1,) * (len(extent) - 1 - axis_at))
    return gain


def bell_draw(key, dims, width, reach, cuts=(), kind=jnp.bfloat16):
    values = width * jax.random.normal(key, dims, jnp.float32)
    if cuts:
        values = values * block_scale(key, dims, cuts, -0.22, 0.18)
    return jnp.clip(values, -reach, reach).astype(kind)


def setup_inputs(seed: int = 0) -> dict:
    seeds = jax.random.split(jax.random.key(seed), 4)
    spectra = bell_draw(seeds[0], (CLIPS, 2, BINS, FRAMES), 1.0, 6.0, ((0, 4), (2, 64)))
    target = draw_target(jax.random.fold_in(seeds[3], 71), 0)
    lengths = draw_lengths(jax.random.fold_in(seeds[3], 71), 0)
    return {"spectra": spectra, "target": target, "lengths": lengths}


EPS_MAG = 0.1
EPS_RATIO = 1e-05

def wave_table(bins_index, time_index, points, factor):
    halfway = points // 2
    is_sine = bins_index >= halfway
    harmonic = jnp.where(is_sine, bins_index - halfway, bins_index)
    angles = (harmonic * time_index % points).astype(jnp.float32) * (2.0 * math.pi / points)
    window = 0.5 - 0.5 * jnp.cos(time_index.astype(jnp.float32) * (2.0 * math.pi / points))
    entry_value = jnp.where(is_sine, -jnp.sin(angles), jnp.cos(angles))
    return (entry_value * window * factor).astype(jnp.bfloat16)

def frame_rows(signal, points):
    stride = points // 4
    frame_count = signal.shape[0] // stride
    padded = jnp.concatenate([signal, jnp.zeros((3 * stride,), signal.dtype)]).reshape(frame_count + 3, stride)
    return jnp.concatenate([padded[quarter:quarter + frame_count] for quarter in range(4)], axis=1)

def intersection_rows(framed, points):
    stride = points // 4
    frame_count = framed.shape[0]
    summed = sum((jnp.pad(framed[:, quarter * stride:(quarter + 1) * stride], ((quarter, 3 - quarter), (0, 0))) for quarter in range(4)))
    return summed[:frame_count].reshape(frame_count * stride)

def one_clip(spectrum, recorded, length):
    synthesis = wave_table(jnp.arange(2 * BINS).astype(jnp.int32)[:, None], jnp.arange(NFFT).astype(jnp.int32)[None, :], NFFT, 1.0 / math.sqrt(BINS))
    stacked = spectrum.reshape(2 * BINS, FRAMES)
    signals = jnp.dot(stacked.T, synthesis, preferred_element_type=jnp.float32)
    sample_index = jnp.arange(SAMPLES).astype(jnp.int32)
    inside = sample_index < length * HOP
    estimate = jnp.where(inside, intersection_rows(signals, NFFT), 0.0).astype(jnp.bfloat16)
    clean = jnp.where(inside, recorded, jnp.zeros_like(recorded))
    clip_terms = []
    gradient = jnp.zeros((SAMPLES,), jnp.float32)
    for points in (NFFT // 4, NFFT // 2, NFFT):
        stride = points // 4
        halfway = points // 2
        analysis = wave_table(jnp.arange(points).astype(jnp.int32)[None, :], jnp.arange(points).astype(jnp.int32)[:, None], points, 1.0 / math.sqrt(points))
        est_x = jnp.dot(frame_rows(estimate, points), analysis, preferred_element_type=jnp.float32)
        tgt_x = jnp.dot(frame_rows(clean, points), analysis, preferred_element_type=jnp.float32)
        est_real = est_x[:, :halfway]
        est_imag = est_x[:, halfway:]
        est_mag = jnp.sqrt(est_real * est_real + est_imag * est_imag + EPS_MAG)
        tgt_mag = jnp.sqrt(tgt_x[:, :halfway] * tgt_x[:, :halfway] + tgt_x[:, halfway:] * tgt_x[:, halfway:] + EPS_MAG)
        usable_count = length * (HOP // stride)
        usable = (jnp.arange(SAMPLES // stride).astype(jnp.int32) < usable_count)[:, None]
        mag_gap = est_mag - tgt_mag
        log_gap = jnp.log(est_mag) - jnp.log(tgt_mag)
        spread = jnp.sum(jnp.where(usable, mag_gap * mag_gap, 0.0))
        energy = jnp.sum(jnp.where(usable, tgt_mag * tgt_mag, 0.0))
        entries = (usable_count * halfway).astype(jnp.float32)
        logterm = jnp.sum(jnp.where(usable, log_gap * log_gap, 0.0)) / entries
        clip_terms.append(jnp.sqrt((spread + EPS_RATIO) / energy) + logterm)
        grad_mag = jnp.where(usable, mag_gap / jnp.sqrt((spread + EPS_RATIO) * energy) + 2.0 * log_gap / (est_mag * entries), 0.0) * (FRAMES * BINS)
        grad_x = jnp.concatenate([grad_mag * est_real / est_mag, grad_mag * est_imag / est_mag], axis=1).astype(jnp.bfloat16)
        grad_frames = jnp.dot(grad_x, analysis.T, preferred_element_type=jnp.float32)
        gradient = gradient + intersection_rows(grad_frames, points)
    grad_wave = jnp.where(inside, gradient, 0.0).astype(jnp.bfloat16)
    hop_rows = jnp.concatenate([grad_wave.reshape(FRAMES, HOP), jnp.zeros((3, HOP), jnp.bfloat16)], axis=0)
    grad_signals = jnp.concatenate([hop_rows[quarter:quarter + FRAMES] for quarter in range(4)], axis=1)
    spec_grad = jnp.dot(grad_signals, synthesis.T, preferred_element_type=jnp.float32).T.reshape(2, BINS, FRAMES).astype(jnp.bfloat16)
    return (sum(clip_terms), spec_grad)

def reference(spectra, target, lengths):

    def per_clip(clip_items):
        return one_clip(clip_items[0], clip_items[1], clip_items[2])
    losses, spec_grad = lax.map(per_clip, (spectra, target, lengths))
    return (jnp.sum(losses) / (3 * CLIPS), spec_grad)
```

```python
import math

import jax
import jax.numpy as jnp
import ml_dtypes
import numpy as np
from jax import lax
from jax.sharding import Mesh
from jax.sharding import PartitionSpec as P

BINS = 1024
NFFT = 2048
HOP = 512
SEG = ("seg_0", "seg_1", "seg_2", "seg_3")


EPS_MAG = 0.1
EPS_RATIO = 1e-05


def shifted(block, axis, distance):
    devices = range(lax.axis_size(axis))
    route = [(i - distance, i) for i in devices if i - distance in devices]
    return lax.ppermute(block, axis, route)


def from_everyone(x, axis):
    devices = lax.axis_size(axis)
    return lax.all_to_all(jnp.broadcast_to(x[None], (devices, *x.shape)), axis, 0, 0, tiled=True)


def of_everyone(x, axis):
    return from_everyone(x, axis).sum(axis=0)


def wave_table(bins_index, time_index, points, factor):
    halfway = points // 2
    is_sine = bins_index >= halfway
    harmonic = np.where(is_sine, bins_index - halfway, bins_index)
    angles = (harmonic * time_index % points).astype(np.float32) * np.float32(2.0 * math.pi / points)
    window = np.float32(0.5) - np.float32(0.5) * np.cos(
        time_index.astype(np.float32) * np.float32(2.0 * math.pi / points)
    )
    entry_value = np.where(is_sine, -np.sin(angles), np.cos(angles))
    return (entry_value * window * np.float32(factor)).astype(ml_dtypes.bfloat16)


def analysis_table(points):
    index = np.arange(points, dtype=np.int32)
    return wave_table(index[None, :], index[:, None], points, 1.0 / math.sqrt(points))


def synthesis_table():
    index = np.arange(NFFT, dtype=np.int32)
    return wave_table(index[:, None], index[None, :], NFFT, 1.0 / math.sqrt(BINS))


def spread_parts(quarters):
    return sum(
        (
            jnp.pad(quarters[:, :, quarter], ((0, 0), (quarter, 3 - quarter), (0, 0)))
            for quarter in range(4)
        )
    )


def framed(signal, beyond, stride):
    frame_count = signal.shape[1] // stride
    padded = jnp.concatenate([signal, beyond], axis=1).reshape(
        signal.shape[0], frame_count + 3, stride
    )
    return jnp.concatenate(
        [padded[:, quarter : quarter + frame_count] for quarter in range(4)], axis=2
    )


def body(spectra, target, lengths):
    clip_count = spectra.shape[0]
    frames_all = spectra.shape[3]
    samples = target.shape[1]
    rows_here = samples // HOP
    seg_index = lax.axis_index(SEG)
    start_sample = seg_index * samples
    block = lax.all_to_all(spectra, SEG, split_axis=3, concat_axis=2, tiled=True)
    stacked = block.reshape(block.shape[0], 2 * BINS, block.shape[3])
    synthesis = jnp.asarray(synthesis_table())
    signals = jnp.einsum("ckf,km->cfm", stacked, synthesis, preferred_element_type=jnp.float32)
    spilled = spread_parts(signals.reshape(clip_count, rows_here, 4, HOP))
    spill = shifted(spilled[:, rows_here:], SEG, 1)
    estimate = (
        spilled[:, :rows_here] + jnp.pad(spill, ((0, 0), (0, rows_here - 3), (0, 0)))
    ).reshape(clip_count, samples)
    sample_index = start_sample + jnp.arange(samples, dtype=jnp.int32)
    inside = sample_index[None, :] < (lengths * HOP)[:, None]
    est_wave = jnp.where(inside, estimate, 0.0).astype(jnp.bfloat16)
    clean = jnp.where(inside, target, jnp.zeros_like(target))
    sizes_list = (NFFT // 4, NFFT // 2, NFFT)
    beyond_est, beyond_tgt = shifted((est_wave[:, : 3 * HOP], clean[:, : 3 * HOP]), SEG, -1)
    beyond_list = [
        (beyond_est[:, : 3 * (points // 4)], beyond_tgt[:, : 3 * (points // 4)])
        for points in sizes_list
    ]
    saved = []
    tables = []
    spread_list = []
    energy_list = []
    logterm_list = []
    for points, beyond_pair in zip(sizes_list, beyond_list):
        stride = points // 4
        halfway = points // 2
        frame_count = samples // stride
        paired = jnp.stack(
            [framed(est_wave, beyond_pair[0], stride), framed(clean, beyond_pair[1], stride)]
        )
        analysis = jnp.asarray(analysis_table(points))
        tables.append(analysis)
        spectra_pair = jnp.einsum(
            "ecfm,mj->ecfj", paired, analysis, preferred_element_type=jnp.float32
        )
        est_real = spectra_pair[0, :, :, :halfway]
        est_imag = spectra_pair[0, :, :, halfway:]
        tgt_real = spectra_pair[1, :, :, :halfway]
        tgt_imag = spectra_pair[1, :, :, halfway:]
        est_mag = jnp.sqrt(est_real * est_real + est_imag * est_imag + EPS_MAG)
        tgt_mag = jnp.sqrt(tgt_real * tgt_real + tgt_imag * tgt_imag + EPS_MAG)
        usable_count = lengths * (HOP // stride)
        frame_index = start_sample // stride + jnp.arange(frame_count, dtype=jnp.int32)
        usable = frame_index[None, :, None] < usable_count[:, None, None]
        mag_gap = est_mag - tgt_mag
        log_gap = jnp.log(est_mag) - jnp.log(tgt_mag)
        entries = (usable_count * halfway).astype(jnp.float32)
        spread_list.append(jnp.sum(jnp.where(usable, mag_gap * mag_gap, 0.0), axis=(1, 2)))
        energy_list.append(jnp.sum(jnp.where(usable, tgt_mag * tgt_mag, 0.0), axis=(1, 2)))
        logterm_list.append(
            jnp.sum(jnp.where(usable, log_gap * log_gap, 0.0), axis=(1, 2)) / entries
        )
        saved.append((est_real, est_imag, est_mag, mag_gap, log_gap, usable, entries))
    spreads = jnp.stack(spread_list)
    energies = jnp.stack(energy_list)
    logterms = jnp.stack(logterm_list)
    spreads, energies, logterms = lax.psum(jnp.stack([spreads, energies, logterms]), SEG)
    own_loss = jnp.sum(jnp.sqrt((spreads + EPS_RATIO) / energies) + logterms)
    loss = of_everyone(own_loss, "clip") / (3 * clip_count * lax.axis_size("clip"))
    ratio_weight = 1.0 / jnp.sqrt((spreads + EPS_RATIO) * energies)
    gradient = jnp.zeros((clip_count, samples), jnp.float32)
    extras = []
    for level, points in enumerate(sizes_list):
        stride = points // 4
        frame_count = samples // stride
        est_real, est_imag, est_mag, mag_gap, log_gap, usable, entries = saved[level]
        grad_mag = jnp.where(
            usable,
            mag_gap * ratio_weight[level][:, None, None]
            + 2.0 * log_gap / (est_mag * entries[:, None, None]),
            0.0,
        ) * (frames_all * BINS)
        grad_x = jnp.concatenate(
            [grad_mag * est_real / est_mag, grad_mag * est_imag / est_mag], axis=2
        ).astype(jnp.bfloat16)
        grad_frames = jnp.einsum(
            "cfj,mj->cfm", grad_x, tables[level], preferred_element_type=jnp.float32
        )
        spread_back = spread_parts(grad_frames.reshape(clip_count, frame_count, 4, stride))
        gradient = gradient + spread_back[:, :frame_count].reshape(clip_count, samples)
        extras.append(spread_back[:, frame_count:].reshape(clip_count, 3 * stride))
    joined = sum(
        (jnp.pad(portion, ((0, 0), (0, 3 * HOP - portion.shape[1]))) for portion in extras)
    )
    received = shifted(joined, SEG, 1)
    gradient = gradient + jnp.pad(received, ((0, 0), (0, samples - 3 * HOP)))
    grad_wave = jnp.where(inside, gradient, 0.0).astype(jnp.bfloat16)
    grad_hops = grad_wave.reshape(clip_count, rows_here, HOP)
    following = shifted(grad_hops[:, :3], SEG, -1)
    extended = jnp.concatenate([grad_hops, following], axis=1)
    grad_signals = jnp.concatenate(
        [extended[:, quarter : quarter + rows_here] for quarter in range(4)], axis=2
    )
    grad_time = jnp.einsum(
        "cfm,km->ckf", grad_signals, synthesis, preferred_element_type=jnp.float32
    )
    rounded = grad_time.reshape(clip_count, 2, BINS, rows_here).astype(jnp.bfloat16)
    spec_grad = lax.all_to_all(rounded, SEG, split_axis=2, concat_axis=3, tiled=True)
    return (loss, spec_grad)


def solution(mesh):
    finer = Mesh(
        mesh.devices.reshape(mesh.shape["clip"], 4, 4, 2, 2),
        ("clip", "seg_0", "seg_1", "seg_2", "seg_3"),
    )
    placed = (P("clip", None, SEG, None), P("clip", SEG), P("clip"))
    return jax.shard_map(
        body,
        mesh=finer,
        in_specs=placed,
        out_specs=(P(), P("clip", None, SEG, None)),
        check_vma=False,
    )
```

```python
import math

import jax
import jax.numpy as jnp
import ml_dtypes
import numpy as np
from jax import lax
from jax.experimental import pallas as pl
from jax.experimental.pallas import tpu as pltpu
from jax.sharding import PartitionSpec as P

BINS = 1024
NFFT = 2048
HOP = 512
FRAMES = 1536
CLIPS = 16
SEGS = 64
CLIP_GROUPS = 4
LOCAL_CLIPS = 4
HOPS = 24
ROWS = 128
SLABS = 16
EPS_MAG = 0.1
EPS_RATIO = 1e-05
SIZES = (512, 1024, 2048)
SCALE = float(FRAMES * BINS)
F32 = jnp.float32
BF16 = jnp.bfloat16
MESH = pl.DeviceIdType.MESH


def wave_table(bins_index, time_index, points, factor):
    halfway = points // 2
    is_sine = bins_index >= halfway
    harmonic = np.where(is_sine, bins_index - halfway, bins_index)
    angles = (harmonic * time_index % points).astype(np.float32) * np.float32(2.0 * math.pi / points)
    window = np.float32(0.5) - np.float32(0.5) * np.cos(
        time_index.astype(np.float32) * np.float32(2.0 * math.pi / points)
    )
    entry_value = np.where(is_sine, -np.sin(angles), np.cos(angles))
    return (entry_value * window * np.float32(factor)).astype(ml_dtypes.bfloat16)


def analysis_table(points):
    index = np.arange(points, dtype=np.int32)
    return wave_table(index[None, :], index[:, None], points, 1.0 / math.sqrt(points))


def synthesis_table():
    owner, part, bin_at = np.meshgrid(np.arange(64), np.arange(2), np.arange(16), indexing="ij")
    index = (part * BINS + owner * 16 + bin_at).reshape(-1).astype(np.int32)
    time = np.arange(NFFT, dtype=np.int32)
    return wave_table(index[:, None], time[None, :], NFFT, 1.0 / math.sqrt(BINS))


def to_seg(index):
    return {"seg": index}


def matmul(a, b):
    return lax.dot_general(a, b, (((1,), (0,)), ((), ())), preferred_element_type=F32)


def matmul_nt(a, b):
    return lax.dot_general(a, b, (((1,), (1,)), ((), ())), preferred_element_type=F32)


def swap_lane_groups(tiles):
    lane = lax.broadcasted_iota(jnp.int32, tiles[0].shape, 1) // 32
    results = []
    for j in range(4):
        result = tiles[j]
        for i in range(4):
            if i != j:
                moved = pltpu.roll(tiles[i], (32 * (i - j)) % 128, 1)
                result = jnp.where(lane == i, moved, result)
        results.append(result)
    return results


def overlap_add(windows):
    total = windows[:, :HOP]
    for q in range(1, 4):
        total = total + pltpu.roll(windows[:, q * HOP : (q + 1) * HOP], q, 0)
    return total


def write_windows(windows_ref, wave):
    windows_ref[:, :HOP] = wave.astype(BF16)
    for q in range(1, 4):
        windows_ref[:, q * HOP : (q + 1) * HOP] = pltpu.roll(wave, ROWS - q, 0).astype(BF16)


def fold_rows(tile):
    by_clip = tile.reshape(LOCAL_CLIPS, 4, 8, tile.shape[1]).sum(axis=1)
    return by_clip[:, :, :128] + by_clip[:, :, 128:]


def kernel(
    spec_ref, target_ref, lengths_ref, syn_hbm, a512_hbm, a1024_hbm, a2048_hbm,
    out_ref, loss_ref,
    send_in, recv_in, chunk_in, send_out, recv_out,
    syn, a512, a1024, a2048,
    tgt, tgt_win, est_own, est_tail, est_head, est_win,
    windows, tgt_mag, tgt_log, est_x, mag_part, log_part, grad_x,
    grad_own, grad_tail, grad_head, grad_win,
    sums, stat_send, stat_recv, loss_send, loss_recv,
    table_sem, in_send_sem, in_recv_sem, out_send_sem, out_recv_sem,
    tgt_sem, est_sem, grad_sem, stat_sem, loss_sem,
):
    me = lax.axis_index("seg")
    clip = lax.axis_index("clip")
    after = lax.rem(me + 1, SEGS)
    before = lax.rem(me + SEGS - 1, SEGS)
    analysis = (a512, a1024, a2048)

    barrier = pltpu.get_barrier_semaphore()

    def greet(step, carry):
        pl.semaphore_signal(
            barrier, inc=1, device_id=to_seg(lax.rem(me + step, SEGS)), device_id_type=MESH
        )
        return carry

    lax.fori_loop(1, SEGS, greet, 0)
    for step in range(1, CLIP_GROUPS):
        pl.semaphore_signal(
            barrier,
            inc=1,
            device_id={"clip": lax.rem(clip + step, CLIP_GROUPS)},
            device_id_type=MESH,
        )

    table_copies = [
        pltpu.make_async_copy(source, held, table_sem.at[at])
        for at, (source, held) in enumerate(
            ((a512_hbm, a512), (a1024_hbm, a1024), (a2048_hbm, a2048), (syn_hbm, syn))
        )
    ]
    for copy in table_copies:
        copy.start()

    for part in range(4):
        turned = spec_ref[:, 384 * part : 384 * (part + 1)].astype(F32).T
        send_in[16 * part : 16 * (part + 1)] = turned.reshape(16, HOPS, 128).astype(BF16)
    for hop in range(HOPS):
        tgt[:, hop, :] = target_ref[:, hop * HOP : (hop + 1) * HOP].astype(F32)

    pl.semaphore_wait(barrier, SEGS - 1 + CLIP_GROUPS - 1)

    tgt_copy = pltpu.make_async_remote_copy(
        src_ref=tgt.at[:, pl.ds(0, 8), :],
        dst_ref=tgt.at[:, pl.ds(HOPS, 8), :],
        send_sem=tgt_sem.at[0],
        recv_sem=tgt_sem.at[1],
        device_id=to_seg(before),
        device_id_type=MESH,
    )
    tgt_copy.start()

    my_chunk = me // SLABS

    def send_bins(step, carry):
        there = lax.rem(me + step, SEGS)
        pltpu.make_async_remote_copy(
            src_ref=send_in.at[there],
            dst_ref=recv_in.at[me],
            send_sem=in_send_sem,
            recv_sem=in_recv_sem.at[my_chunk],
            device_id=to_seg(there),
            device_id_type=MESH,
        ).start()
        return carry

    lax.fori_loop(1, SEGS, send_bins, 0)
    pltpu.make_async_copy(send_in.at[me], recv_in.at[me], in_recv_sem.at[my_chunk]).start()

    row = lax.broadcasted_iota(jnp.int32, (ROWS, 1), 0)
    row_clip = row // 32
    row_hop = lax.rem(row, 32)
    row_length = jnp.full((ROWS, 1), lengths_ref[0], jnp.int32)
    for c in range(1, LOCAL_CLIPS):
        row_length = jnp.where(row_clip == c, lengths_ref[c], row_length)
    inside = me * HOPS + row_hop < row_length
    usable = inside & (row_hop < HOPS)

    tgt_copy.wait()
    write_windows(tgt_win, jnp.where(inside, tgt[...].reshape(ROWS, HOP), 0.0))
    for level, points in enumerate(SIZES):
        half = points // 2
        stride = points // 4
        table_copies[level].wait()
        for at in range(HOP // stride):
            rows = pl.ds(at * ROWS, ROWS)

            def target_columns(step, energy, level=level, points=points, half=half, at=at):
                column = pl.multiple_of(step * 256, 256)
                frames = tgt_win[:, at * (points // 4) : at * (points // 4) + points]
                real = matmul(frames, analysis[level][:, pl.ds(column, 256)])
                imag = matmul(frames, analysis[level][:, pl.ds(half + column, 256)])
                power = real * real + imag * imag + EPS_MAG
                place = pl.ds(pl.multiple_of(at * half + column, 256), 256)
                tgt_mag[level, :, place] = jnp.sqrt(power)
                tgt_log[level, :, place] = 0.5 * jnp.log(power)
                return energy + fold_rows(jnp.where(usable, power, 0.0))

            start = jnp.zeros((LOCAL_CLIPS, 8, 128), F32)
            found = lax.fori_loop(0, half // 256, target_columns, start)
            if at == 0:
                sums[3 + level] = found
            else:
                sums[3 + level] = sums[3 + level] + found

    table_copies[3].wait()
    for turn in range(4):
        chunk = lax.rem(my_chunk + (4 - turn), 4)
        slabs = pl.ds(pl.multiple_of(chunk * SLABS, SLABS), SLABS)
        pltpu.make_async_copy(
            send_in.at[slabs], recv_in.at[slabs], in_recv_sem.at[chunk]
        ).wait()
        arrived = recv_in[slabs].astype(F32).reshape(4, 4, HOPS, 128)
        by_source = [arrived[:, i].reshape(4 * HOPS, 128) for i in range(4)]
        by_clip = swap_lane_groups(by_source)
        for c in range(LOCAL_CLIPS):
            for g in range(4):
                block = by_clip[c][g * HOPS : (g + 1) * HOPS]
                block = jnp.concatenate([block, jnp.zeros((8, 128), F32)], axis=0)
                chunk_in[c * 32 : (c + 1) * 32, g * 128 : (g + 1) * 128] = block.astype(BF16)
        for tile in range(4):
            columns = slice(tile * 512, (tile + 1) * 512)
            product = matmul(
                chunk_in[...], syn[pl.ds(pl.multiple_of(chunk * 512, 512), 512), columns]
            )
            if turn == 0:
                windows[:, columns] = product
            else:
                windows[:, columns] = windows[:, columns] + product

    def neighbours(own, tail, head, sem):
        return (
            pltpu.make_async_remote_copy(
                src_ref=own.at[:, pl.ds(HOPS, 8), :],
                dst_ref=tail,
                send_sem=sem.at[0],
                recv_sem=sem.at[1],
                device_id=to_seg(after),
                device_id_type=MESH,
            ),
            pltpu.make_async_remote_copy(
                src_ref=own.at[:, pl.ds(0, 8), :],
                dst_ref=head,
                send_sem=sem.at[2],
                recv_sem=sem.at[3],
                device_id=to_seg(before),
                device_id_type=MESH,
            ),
        )

    def joined(own, tail, head):
        first = jnp.where(me == 0, 0.0, tail[...])
        hop = lax.broadcasted_iota(jnp.int32, head.shape, 1)
        last = jnp.where(hop < 3, head[...], 0.0)
        whole = jnp.concatenate(
            [own[:, :8] + first, own[:, 8:HOPS], own[:, HOPS:] + last], axis=1
        )
        return jnp.where(inside, whole.reshape(ROWS, HOP), 0.0)

    est_own[...] = overlap_add(windows[...]).reshape(LOCAL_CLIPS, 32, HOP)
    est_copies = neighbours(est_own, est_tail, est_head, est_sem)
    for copy in est_copies:
        copy.start()
    for copy in est_copies:
        copy.wait()
    write_windows(est_win, joined(est_own, est_tail, est_head))

    for level, points in enumerate(SIZES):
        half = points // 2
        stride = points // 4
        for at in range(HOP // stride):

            def columns(step, carry, level=level, points=points, half=half, at=at):
                spread, logterm = carry
                column = pl.multiple_of(step * 256, 256)
                frames = est_win[:, at * (points // 4) : at * (points // 4) + points]
                real = matmul(frames, analysis[level][:, pl.ds(column, 256)])
                imag = matmul(frames, analysis[level][:, pl.ds(half + column, 256)])
                power = real * real + imag * imag + EPS_MAG
                inverse = lax.rsqrt(power)
                place = pl.ds(pl.multiple_of(at * half + column, 256), 256)
                gap = power * inverse - tgt_mag[level, :, place]
                log_gap = 0.5 * jnp.log(power) - tgt_log[level, :, place]
                est_x[level, 0, :, place] = real
                est_x[level, 1, :, place] = imag
                mag_part[level, :, place] = gap * inverse
                log_part[level, :, place] = log_gap * inverse * inverse
                return (
                    spread + fold_rows(jnp.where(usable, gap * gap, 0.0)),
                    logterm + fold_rows(jnp.where(usable, log_gap * log_gap, 0.0)),
                )

            start = jnp.zeros((LOCAL_CLIPS, 8, 128), F32)
            spread, logterm = lax.fori_loop(0, half // 256, columns, (start, start))
            if at == 0:
                sums[level] = spread
                sums[6 + level] = logterm
            else:
                sums[level] = sums[level] + spread
                sums[6 + level] = sums[6 + level] + logterm

    flat = sums[...].reshape(36, 8, 128).sum(axis=1)
    flat = jnp.sum(flat, axis=1, keepdims=True)
    lane = lax.broadcasted_iota(jnp.int32, (36, 128), 1)
    line = lax.broadcasted_iota(jnp.int32, (36, 128), 0)
    own_stats = jnp.sum(jnp.where(lane == line, flat, 0.0), axis=0, keepdims=True)
    stat_send[...] = own_stats
    stat_recv[me] = own_stats

    def send_stats(step, carry):
        pltpu.make_async_remote_copy(
            src_ref=stat_send,
            dst_ref=stat_recv.at[me],
            send_sem=stat_sem.at[0],
            recv_sem=stat_sem.at[1],
            device_id=to_seg(lax.rem(me + step, SEGS)),
            device_id_type=MESH,
        ).start()
        return carry

    lax.fori_loop(1, SEGS, send_stats, 0)
    others = stat_recv.at[pl.ds(0, SEGS - 1)]
    pltpu.make_async_copy(others, others, stat_sem.at[1]).wait()
    pltpu.make_async_copy(others, others, stat_sem.at[0]).wait()
    totals = stat_recv[...].sum(axis=0)

    energy = pltpu.roll(totals, 128 - 12, 1)
    logterm = pltpu.roll(totals, 128 - 24, 1)
    place = lax.broadcasted_iota(jnp.int32, (1, 128), 1)
    filled = place < 12
    lane_length = jnp.full((1, 128), lengths_ref[0], jnp.int32)
    for c in range(1, LOCAL_CLIPS):
        lane_length = jnp.where(lax.rem(place, 4) == c, lengths_ref[c], lane_length)
    entries = (lane_length * BINS).astype(F32)
    safe_energy = jnp.where(filled, energy, 1.0)
    safe_spread = jnp.where(filled, totals, 1.0) + EPS_RATIO
    terms = jnp.where(filled, jnp.sqrt(safe_spread / safe_energy) + logterm / entries, 0.0)
    own_loss = jnp.sum(terms, axis=1, keepdims=True) + jnp.zeros((1, 128), F32)
    loss_send[...] = own_loss
    loss_recv[clip] = own_loss
    for step in range(1, CLIP_GROUPS):
        pltpu.make_async_remote_copy(
            src_ref=loss_send,
            dst_ref=loss_recv.at[clip],
            send_sem=loss_sem.at[0],
            recv_sem=loss_sem.at[1],
            device_id={"clip": lax.rem(clip + step, CLIP_GROUPS)},
            device_id_type=MESH,
        ).start()

    weights = SCALE / jnp.sqrt(safe_spread * safe_energy)
    weights = jnp.broadcast_to(weights, (ROWS, 128))
    pick_lane = lax.broadcasted_iota(jnp.int32, (ROWS, 128), 1)
    pick_row = lax.broadcasted_iota(jnp.int32, (ROWS, 128), 0) // 32
    log_weight = (2.0 * SCALE) / (row_length * BINS).astype(F32)
    for level, points in enumerate(SIZES):
        half = points // 2
        mag_weight = jnp.sum(
            jnp.where(pick_lane == level * 4 + pick_row, weights, 0.0), axis=1, keepdims=True
        )
        for at in range(2048 // points):

            def gradients(step, carry, level=level, half=half, at=at, mag_weight=mag_weight):
                column = pl.multiple_of(step * 256, 256)
                place = pl.ds(pl.multiple_of(at * half + column, 256), 256)
                factor = jnp.where(
                    usable,
                    mag_part[level, :, place] * mag_weight + log_part[level, :, place] * log_weight,
                    0.0,
                )
                first = pl.multiple_of(at * 2 * half + column, 256)
                second = pl.multiple_of(at * 2 * half + half + column, 256)
                grad_x[level, :, pl.ds(first, 256)] = (factor * est_x[level, 0, :, place]).astype(BF16)
                grad_x[level, :, pl.ds(second, 256)] = (factor * est_x[level, 1, :, place]).astype(BF16)
                return carry

            lax.fori_loop(0, half // 256, gradients, 0)

    def back(step, carry):
        column = pl.multiple_of(step * 256, 256)
        windows[:, pl.ds(column, 256)] = matmul_nt(grad_x[2], a2048[pl.ds(column, 256), :])
        return carry

    lax.fori_loop(0, 8, back, 0)
    for level, points in ((1, 1024), (0, 512)):
        for at in range(2048 // points):
            for step in range(points // 256):
                first = at * (points // 4) + step * 256
                product = matmul_nt(
                    grad_x[level, :, at * points : (at + 1) * points],
                    analysis[level][step * 256 : (step + 1) * 256, :],
                )
                windows[:, first : first + 256] = windows[:, first : first + 256] + product

    grad_own[...] = overlap_add(windows[...]).reshape(LOCAL_CLIPS, 32, HOP)
    grad_copies = neighbours(grad_own, grad_tail, grad_head, grad_sem)
    for copy in grad_copies:
        copy.start()
    for copy in grad_copies:
        copy.wait()
    write_windows(grad_win, joined(grad_own, grad_tail, grad_head))

    first_tile = me // 8 + 1

    def back_bins(step, carry):
        tile = lax.rem(first_tile + step, 8)
        product = matmul_nt(grad_win[...], syn[pl.ds(pl.multiple_of(tile * 256, 256), 256), :])
        for g in range(2):
            lanes = product[:, g * 128 : (g + 1) * 128]
            by_clip = [lanes[c * 32 : c * 32 + HOPS] for c in range(LOCAL_CLIPS)]
            for i, block in enumerate(swap_lane_groups(by_clip)):
                send_out[tile * 8 + g * 4 + i] = block.astype(BF16)
        for i in range(8):
            there = tile * 8 + i

            @pl.when(there != me)
            def _():
                pltpu.make_async_remote_copy(
                    src_ref=send_out.at[there],
                    dst_ref=recv_out.at[me],
                    send_sem=out_send_sem,
                    recv_sem=out_recv_sem.at[my_chunk],
                    device_id=to_seg(there),
                    device_id_type=MESH,
                ).start()

            @pl.when(there == me)
            def _():
                pltpu.make_async_copy(
                    send_out.at[me], recv_out.at[me], out_recv_sem.at[my_chunk]
                ).start()

        return carry

    lax.fori_loop(0, 8, back_bins, 0)

    three = loss_recv.at[pl.ds(0, CLIP_GROUPS - 1)]
    pltpu.make_async_copy(three, three, loss_sem.at[1]).wait()
    pltpu.make_async_copy(three, three, loss_sem.at[0]).wait()
    loss_ref[...] = loss_recv[...].sum(axis=0) / (3 * CLIPS)

    for chunk in range(4):
        slabs = pl.ds(chunk * SLABS, SLABS)
        pltpu.make_async_copy(
            send_out.at[slabs], recv_out.at[slabs], out_recv_sem.at[chunk]
        ).wait()
        turned = recv_out[slabs].astype(F32).reshape(SLABS * HOPS, 128).T
        out_ref[:, chunk * 384 : (chunk + 1) * 384] = turned.astype(BF16)

    sent = pl.ds(0, SEGS - 1)
    pltpu.make_async_copy(send_in.at[sent], recv_in.at[sent], in_send_sem).wait()
    pltpu.make_async_copy(send_out.at[sent], recv_out.at[sent], out_send_sem).wait()


def body(spectra, target, lengths):
    vmem = pl.BlockSpec(memory_space=pltpu.VMEM)
    smem = pl.BlockSpec(memory_space=pltpu.SMEM)
    anywhere = pl.BlockSpec(memory_space=pl.ANY)
    slabs = pltpu.VMEM((SEGS, HOPS, 128), BF16)
    hops8 = pltpu.VMEM((LOCAL_CLIPS, 8, HOP), F32)
    hops32 = pltpu.VMEM((LOCAL_CLIPS, 32, HOP), F32)
    window = pltpu.VMEM((ROWS, NFFT), BF16)
    entries = pltpu.VMEM((3, ROWS, BINS), F32)
    dma = pltpu.SemaphoreType.DMA
    out, loss = pl.pallas_call(
        kernel,
        out_shape=(
            jax.ShapeDtypeStruct((ROWS, FRAMES), BF16),
            jax.ShapeDtypeStruct((1, 128), F32),
        ),
        in_specs=[vmem, vmem, smem] + [anywhere] * 4,
        out_specs=(vmem, vmem),
        scratch_shapes=[
            slabs, slabs, pltpu.VMEM((ROWS, 512), BF16), slabs, slabs,
            pltpu.VMEM((2048, 2048), BF16), pltpu.VMEM((512, 512), BF16),
            pltpu.VMEM((1024, 1024), BF16), pltpu.VMEM((2048, 2048), BF16),
            hops32, window, hops32, hops8, hops8, window,
            pltpu.VMEM((ROWS, NFFT), F32), entries, entries,
            pltpu.VMEM((3, 2, ROWS, BINS), F32), entries, entries,
            pltpu.VMEM((3, ROWS, NFFT), BF16),
            hops32, hops8, hops8, window,
            pltpu.VMEM((9, LOCAL_CLIPS, 8, 128), F32),
            pltpu.VMEM((1, 128), F32), pltpu.VMEM((SEGS, 1, 128), F32),
            pltpu.VMEM((1, 128), F32), pltpu.VMEM((CLIP_GROUPS, 1, 128), F32),
            dma((4,)), dma, dma((4,)), dma, dma((4,)),
            dma((2,)), dma((4,)), dma((4,)), dma((2,)), dma((2,)),
        ],
        compiler_params=pltpu.CompilerParams(
            collective_id=0, has_side_effects=True, vmem_limit_bytes=60 * 2**20
        ),
        cost_estimate=pl.CostEstimate(
            flops=8 * 10**9, bytes_accessed=20 * 10**6, transcendentals=10**6
        ),
    )(
        spectra.reshape(ROWS, FRAMES),
        target,
        lengths,
        jnp.asarray(synthesis_table()),
        *(jnp.asarray(analysis_table(points)) for points in SIZES),
    )
    return loss[0, 0], out.reshape(LOCAL_CLIPS, 2, BINS // SEGS, FRAMES)


def solution(mesh):
    placed = (P("clip", None, "seg", None), P("clip", "seg"), P("clip"))
    return jax.shard_map(
        body,
        mesh=mesh,
        in_specs=placed,
        out_specs=(P(), P("clip", None, "seg", None)),
        check_vma=False,
    )
```

```python
import math

import jax
import jax.numpy as jnp
import ml_dtypes
import numpy as np
from jax import lax
from jax.experimental import pallas as pl
from jax.experimental.pallas import tpu as pltpu
from jax.sharding import PartitionSpec as P

BINS = 1024
NFFT = 2048
HOP = 512
FRAMES = 1536
CLIPS = 16
SEGS = 64
WORKS = 32
CLIP_GROUPS = 4
LOCAL_CLIPS = 4
HOPS = 24
ROWS = 128
SLABS = 16
EPS_MAG = 0.1
EPS_RATIO = 1e-05
SIZES = (512, 1024, 2048)
SCALE = float(FRAMES * BINS)
F32 = jnp.float32
BF16 = jnp.bfloat16
MESH = pl.DeviceIdType.MESH


def wave_table(bins_index, time_index, points, factor):
    halfway = points // 2
    is_sine = bins_index >= halfway
    harmonic = np.where(is_sine, bins_index - halfway, bins_index)
    angles = (harmonic * time_index % points).astype(np.float32) * np.float32(2.0 * math.pi / points)
    window = np.float32(0.5) - np.float32(0.5) * np.cos(
        time_index.astype(np.float32) * np.float32(2.0 * math.pi / points)
    )
    entry_value = np.where(is_sine, -np.sin(angles), np.cos(angles))
    return (entry_value * window * np.float32(factor)).astype(ml_dtypes.bfloat16)


def analysis_table(points):
    index = np.arange(points, dtype=np.int32)
    return wave_table(index[None, :], index[:, None], points, 1.0 / math.sqrt(points))


def synthesis_table():
    owner, part, bin_at = np.meshgrid(np.arange(64), np.arange(2), np.arange(16), indexing="ij")
    index = (part * BINS + owner * 16 + bin_at).reshape(-1).astype(np.int32)
    time = np.arange(NFFT, dtype=np.int32)
    return wave_table(index[:, None], time[None, :], NFFT, 1.0 / math.sqrt(BINS))


def to_seg(index):
    return {"seg": index}


def matmul(a, b):
    return lax.dot_general(a, b, (((1,), (0,)), ((), ())), preferred_element_type=F32)


def matmul_nt(a, b):
    return lax.dot_general(a, b, (((1,), (1,)), ((), ())), preferred_element_type=F32)


def swap_lane_groups(tiles):
    lane = lax.broadcasted_iota(jnp.int32, tiles[0].shape, 1) // 32
    results = []
    for j in range(4):
        result = tiles[j]
        for i in range(4):
            if i != j:
                moved = pltpu.roll(tiles[i], (32 * (i - j)) % 128, 1)
                result = jnp.where(lane == i, moved, result)
        results.append(result)
    return results


def overlap_add(windows):
    total = windows[:, :HOP]
    for q in range(1, 4):
        total = total + pltpu.roll(windows[:, q * HOP : (q + 1) * HOP], q, 0)
    return total


def write_windows(windows_ref, wave):
    windows_ref[:, :HOP] = wave.astype(BF16)
    for q in range(1, 4):
        windows_ref[:, q * HOP : (q + 1) * HOP] = pltpu.roll(wave, ROWS - q, 0).astype(BF16)


def halves(first, second):
    shape = first.shape
    first, second = first.reshape(-1, 128), second.reshape(-1, 128)
    low = lax.broadcasted_iota(jnp.int32, first.shape, 1) < 64
    one = jnp.where(low, first, pltpu.roll(second, 64, 1))
    other = jnp.where(low, pltpu.roll(first, 64, 1), second)
    return one.reshape(shape), other.reshape(shape)


def fold_rows(tile):
    by_clip = tile.reshape(LOCAL_CLIPS, 4, 8, tile.shape[1]).sum(axis=1)
    return by_clip[:, :, :128] + by_clip[:, :, 128:]


def kernel(
    spec_ref, target_ref, lengths_ref, syn_hbm, a512_hbm, a1024_hbm, a2048_hbm,
    out_ref, loss_ref,
    send_in, recv_in, chunk_in, send_out, recv_out, tgt_rows, tgt_raw, tgt_next,
    syn, a512, a1024, a2048,
    tgt, tgt_win, est_own, est_tail, est_head, est_win,
    windows, tgt_mag, tgt_log, est_x, mag_part, log_part, grad_x,
    grad_own, grad_tail, grad_head, grad_win,
    sums, stat_send, stat_recv, loss_send, loss_recv,
    table_sem, in_send_sem, in_recv_sem, out_send_sem, out_recv_sem,
    tgt_sem, est_sem, grad_sem, stat_sem, loss_sem,
):
    me = lax.axis_index("seg")
    clip = lax.axis_index("clip")
    analysis = (a512, a1024, a2048)
    spot = me // 4
    core = lax.rem(me, 2)
    side = lax.rem(me // 2, 2)
    work = spot * 2 + core

    def device_of(work_index, side_index):
        return (work_index // 2) * 4 + side_index * 2 + lax.rem(work_index, 2)

    def slot_of(work_index, side_index):
        return (work_index // 8) * 16 + side_index * 8 + lax.rem(work_index, 8)

    after = device_of(lax.rem(work + 1, WORKS), side)
    before = device_of(lax.rem(work + WORKS - 1, WORKS), side)
    my_slot = slot_of(work, side)
    loss_peers = [
        (lax.rem(clip + step // 2, CLIP_GROUPS), device_of(work, lax.rem(side + step, 2)))
        for step in range(1, 2 * CLIP_GROUPS)
    ]

    barrier = pltpu.get_barrier_semaphore()

    def greet(step, carry):
        pl.semaphore_signal(
            barrier, inc=1, device_id=to_seg(lax.rem(me + step, SEGS)), device_id_type=MESH
        )
        return carry

    lax.fori_loop(1, SEGS, greet, 0)
    for peer in loss_peers[1:]:
        pl.semaphore_signal(barrier, inc=1, device_id=peer, device_id_type=MESH)

    table_copies = [
        pltpu.make_async_copy(source, held, table_sem.at[at])
        for at, (source, held) in enumerate(
            ((a512_hbm, a512), (a1024_hbm, a1024), (a2048_hbm, a2048), (syn_hbm, syn))
        )
    ]
    for copy in table_copies:
        copy.start()

    for hop in range(HOPS):
        tgt_rows[:, hop, :] = target_ref[:, hop * HOP : (hop + 1) * HOP].astype(F32)
    tgt_raw[...] = tgt_rows[...].astype(BF16)
    for part in range(4):
        turned = spec_ref[:, 384 * part : 384 * (part + 1)].astype(F32).T
        turned = turned.reshape(8, 2, HOPS, 128)
        for at, message in enumerate(halves(turned[:, 0], turned[:, 1])):
            first = part * 16 + at * 8
            send_in[first : first + 8] = message.astype(BF16)

    pl.semaphore_wait(barrier, SEGS - 1 + len(loss_peers) - 1)

    def hold(to_side):
        return tgt_raw.at[pl.ds(2 * to_side, 2)], tgt.at[pl.ds(2 * core, 2)]

    across_source, across_place = hold(1 - side)
    tgt_across = pltpu.make_async_remote_copy(
        src_ref=across_source,
        dst_ref=across_place,
        send_sem=tgt_sem.at[0],
        recv_sem=tgt_sem.at[1],
        device_id=to_seg(spot * 4 + (1 - side) * 2 + side),
        device_id_type=MESH,
    )
    tgt_across.start()
    near_source, near_place = hold(side)
    near_stays = core == side

    @pl.when(near_stays)
    def _():
        pltpu.make_async_copy(near_source, near_place, tgt_sem.at[1]).start()

    @pl.when(jnp.logical_not(near_stays))
    def _():
        pltpu.make_async_remote_copy(
            src_ref=near_source,
            dst_ref=near_place,
            send_sem=tgt_sem.at[2],
            recv_sem=tgt_sem.at[1],
            device_id=to_seg(spot * 4 + side * 3),
            device_id_type=MESH,
        ).start()

    ahead = lax.rem(spot * 2 + side + WORKS - 1, WORKS)
    heads = [
        (tgt_rows.at[pl.ds(2 * to_side, 2), pl.ds(0, 8), :], device_of(ahead, to_side))
        for to_side in range(2)
    ]
    for at, (source, there) in enumerate(heads):

        @pl.when((core == 0) & (there != me))
        def _(at=at, source=source, there=there):
            pltpu.make_async_remote_copy(
                src_ref=source,
                dst_ref=tgt_next,
                send_sem=tgt_sem.at[3 + at],
                recv_sem=tgt_sem.at[5],
                device_id=to_seg(there),
                device_id_type=MESH,
            ).start()

        @pl.when((core == 0) & (there == me))
        def _(source=source):
            pltpu.make_async_copy(source, tgt_next, tgt_sem.at[5]).start()

    my_chunk = me // SLABS

    def send_bins(step, carry):
        there = lax.rem(me + step, SEGS)
        pltpu.make_async_remote_copy(
            src_ref=send_in.at[
                slot_of((there // 4) * 2 + lax.rem(there, 2), lax.rem(there // 2, 2))
            ],
            dst_ref=recv_in.at[me],
            send_sem=in_send_sem,
            recv_sem=in_recv_sem.at[my_chunk],
            device_id=to_seg(there),
            device_id_type=MESH,
        ).start()
        return carry

    lax.fori_loop(1, SEGS, send_bins, 0)
    pltpu.make_async_copy(send_in.at[my_slot], recv_in.at[me], in_recv_sem.at[my_chunk]).start()

    row = lax.broadcasted_iota(jnp.int32, (ROWS, 1), 0)
    row_clip = row // 32
    row_hop = lax.rem(row, 32)
    row_length = jnp.where(
        lax.rem(row_clip, 2) == 0, lengths_ref[2 * side], lengths_ref[2 * side + 1]
    )
    inside = work * (2 * HOPS) + (row_clip // 2) * HOPS + row_hop < row_length
    usable = inside & (row_hop < HOPS)

    pltpu.make_async_copy(tgt_raw, tgt, tgt_sem.at[1]).wait()
    pltpu.make_async_copy(tgt_next, tgt_next, tgt_sem.at[5]).wait()
    own = tgt[...].astype(F32)
    first_half = jnp.concatenate([own[:2], own[2:, :8]], axis=1)
    second_half = jnp.concatenate([own[2:], tgt_next[...]], axis=1)
    own = jnp.concatenate([first_half, second_half], axis=0).reshape(ROWS, HOP)
    write_windows(tgt_win, jnp.where(inside, own, 0.0))

    def frames_of(windows_ref, points):
        stride = points // 4
        parts = [
            windows_ref[:, at * stride : at * stride + points] for at in range(HOP // stride)
        ]
        return parts[0] if len(parts) == 1 else jnp.concatenate(parts, axis=0)

    for level, points in enumerate(SIZES):
        half = points // 2
        count = NFFT // points
        table_copies[level].wait()

        def target_columns(step, energy, level=level, points=points, half=half, count=count):
            column = pl.multiple_of(step * 256, 256)
            frames = frames_of(tgt_win, points)
            real = matmul(frames, analysis[level][:, pl.ds(column, 256)])
            imag = matmul(frames, analysis[level][:, pl.ds(half + column, 256)])
            power = real * real + imag * imag + EPS_MAG
            for at in range(count):
                place = pl.ds(pl.multiple_of(at * half + column, 256), 256)
                part = power[at * ROWS : (at + 1) * ROWS]
                tgt_mag[level, :, place] = jnp.sqrt(part)
                tgt_log[level, :, place] = 0.5 * jnp.log(part)
                energy = energy + fold_rows(jnp.where(usable, part, 0.0))
            return energy

        start = jnp.zeros((LOCAL_CLIPS, 8, 128), F32)
        sums[3 + level] = lax.fori_loop(0, half // 256, target_columns, start)

    table_copies[3].wait()
    for turn in range(4):
        chunk = lax.rem(my_chunk + (4 - turn), 4)
        slabs = pl.ds(pl.multiple_of(chunk * SLABS, SLABS), SLABS)
        pltpu.make_async_copy(
            send_in.at[slabs], recv_in.at[slabs], in_recv_sem.at[chunk]
        ).wait()
        arrived = recv_in[slabs].astype(F32).reshape(4, 4, HOPS, 128)
        by_source = [arrived[:, i].reshape(4 * HOPS, 128) for i in range(4)]
        by_clip = swap_lane_groups(by_source)
        for c in range(LOCAL_CLIPS):
            for g in range(4):
                block = by_clip[c][g * HOPS : (g + 1) * HOPS]
                block = jnp.concatenate([block, jnp.zeros((8, 128), F32)], axis=0)
                chunk_in[c * 32 : (c + 1) * 32, g * 128 : (g + 1) * 128] = block.astype(BF16)
        for tile in range(4):
            columns = slice(tile * 512, (tile + 1) * 512)
            product = matmul(
                chunk_in[...], syn[pl.ds(pl.multiple_of(chunk * 512, 512), 512), columns]
            )
            if turn == 0:
                windows[:, columns] = product
            else:
                windows[:, columns] = windows[:, columns] + product

    def neighbours(own, tail, head, sem):
        return (
            pltpu.make_async_remote_copy(
                src_ref=own.at[pl.ds(2, 2), pl.ds(HOPS, 8), :],
                dst_ref=tail,
                send_sem=sem.at[0],
                recv_sem=sem.at[1],
                device_id=to_seg(after),
                device_id_type=MESH,
            ),
            pltpu.make_async_remote_copy(
                src_ref=own.at[pl.ds(0, 2), pl.ds(0, 8), :],
                dst_ref=head,
                send_sem=sem.at[2],
                recv_sem=sem.at[3],
                device_id=to_seg(before),
                device_id_type=MESH,
            ),
        )

    def joined(own, tail, head):
        before_us = jnp.where(work == 0, 0.0, tail[...])
        hop = lax.broadcasted_iota(jnp.int32, head.shape, 1)
        after_us = jnp.where(hop < 3, head[...], 0.0)
        one, two = own[:2], own[2:]
        spill = one[:, HOPS:]
        middle = jnp.where(hop < 3, spill + two[:, :8], 0.0)
        one = jnp.concatenate([one[:, :8] + before_us, one[:, 8:HOPS], middle], axis=1)
        two = jnp.concatenate(
            [two[:, :8] + spill, two[:, 8:HOPS], two[:, HOPS:] + after_us], axis=1
        )
        whole = jnp.concatenate([one, two], axis=0)
        return jnp.where(inside, whole.reshape(ROWS, HOP), 0.0)

    est_own[...] = overlap_add(windows[...]).reshape(LOCAL_CLIPS, 32, HOP)
    est_copies = neighbours(est_own, est_tail, est_head, est_sem)
    for copy in est_copies:
        copy.start()
    for copy in est_copies:
        copy.wait_recv()
    write_windows(est_win, joined(est_own, est_tail, est_head))

    for level, points in enumerate(SIZES):
        half = points // 2
        count = NFFT // points
        spread = jnp.zeros((LOCAL_CLIPS, 8, 128), F32)
        logterm = jnp.zeros((LOCAL_CLIPS, 8, 128), F32)
        for column in range(0, half, 256):
            frames = frames_of(est_win, points)
            all_real = matmul(frames, analysis[level][:, column : column + 256])
            all_imag = matmul(frames, analysis[level][:, half + column : half + column + 256])
            for at in range(count):
                rows = slice(at * ROWS, (at + 1) * ROWS)
                real, imag = all_real[rows], all_imag[rows]
                power = real * real + imag * imag + EPS_MAG
                inverse = lax.rsqrt(power)
                place = slice(at * half + column, at * half + column + 256)
                gap = power * inverse - tgt_mag[level, :, place]
                log_gap = 0.5 * jnp.log(power) - tgt_log[level, :, place]
                est_x[level, 0, :, place] = real
                est_x[level, 1, :, place] = imag
                mag_part[level, :, place] = gap * inverse
                log_part[level, :, place] = log_gap * inverse * inverse
                spread = spread + fold_rows(jnp.where(usable, gap * gap, 0.0))
                logterm = logterm + fold_rows(jnp.where(usable, log_gap * log_gap, 0.0))
        sums[level] = spread
        sums[6 + level] = logterm

    flat = sums[...].reshape(36, 8, 128).sum(axis=1)
    flat = jnp.sum(flat, axis=1, keepdims=True)
    lane = lax.broadcasted_iota(jnp.int32, (36, 128), 1)
    line = lax.broadcasted_iota(jnp.int32, (36, 128), 0)
    own_stats = jnp.sum(jnp.where(lane == line, flat, 0.0), axis=0, keepdims=True)
    stat_send[...] = own_stats
    stat_recv[work] = own_stats

    def send_stats(step, carry):
        pltpu.make_async_remote_copy(
            src_ref=stat_send,
            dst_ref=stat_recv.at[work],
            send_sem=stat_sem.at[0],
            recv_sem=stat_sem.at[1],
            device_id=to_seg(device_of(lax.rem(work + step, WORKS), side)),
            device_id_type=MESH,
        ).start()
        return carry

    lax.fori_loop(1, WORKS, send_stats, 0)
    others = stat_recv.at[pl.ds(0, WORKS - 1)]
    pltpu.make_async_copy(others, others, stat_sem.at[1]).wait()
    totals = stat_recv[...].sum(axis=0)

    place = lax.broadcasted_iota(jnp.int32, (1, 128), 1)
    low_half = lax.rem(place, 4) < 2
    totals = totals + jnp.where(low_half, pltpu.roll(totals, 126, 1), pltpu.roll(totals, 2, 1))
    energy = pltpu.roll(totals, 128 - 12, 1)
    logterm = pltpu.roll(totals, 128 - 24, 1)
    filled = place < 12
    lane_length = jnp.where(
        lax.rem(place, 2) == 0, lengths_ref[2 * side], lengths_ref[2 * side + 1]
    )
    entries = (lane_length * BINS).astype(F32)
    safe_energy = jnp.where(filled, energy, 1.0)
    safe_spread = jnp.where(filled, totals, 1.0) + EPS_RATIO
    terms = jnp.where(filled & low_half, jnp.sqrt(safe_spread / safe_energy) + logterm / entries, 0.0)
    own_loss = jnp.sum(terms, axis=1, keepdims=True) + jnp.zeros((1, 128), F32)
    loss_send[...] = own_loss
    my_loss = clip * 2 + side
    loss_recv[my_loss] = own_loss
    for peer in loss_peers:
        pltpu.make_async_remote_copy(
            src_ref=loss_send,
            dst_ref=loss_recv.at[my_loss],
            send_sem=loss_sem.at[0],
            recv_sem=loss_sem.at[1],
            device_id=peer,
            device_id_type=MESH,
        ).start()

    weights = SCALE / jnp.sqrt(safe_spread * safe_energy)
    weights = jnp.broadcast_to(weights, (ROWS, 128))
    pick_lane = lax.broadcasted_iota(jnp.int32, (ROWS, 128), 1)
    pick_row = lax.broadcasted_iota(jnp.int32, (ROWS, 128), 0) // 32
    log_weight = (2.0 * SCALE) / (row_length * BINS).astype(F32)
    for level, points in enumerate(SIZES):
        half = points // 2
        mag_weight = jnp.sum(
            jnp.where(pick_lane == level * 4 + pick_row, weights, 0.0), axis=1, keepdims=True
        )
        for at in range(2048 // points):

            def gradients(step, carry, level=level, half=half, at=at, mag_weight=mag_weight):
                column = pl.multiple_of(step * 256, 256)
                place = pl.ds(pl.multiple_of(at * half + column, 256), 256)
                factor = jnp.where(
                    usable,
                    mag_part[level, :, place] * mag_weight + log_part[level, :, place] * log_weight,
                    0.0,
                )
                first = pl.multiple_of(at * 2 * half + column, 256)
                second = pl.multiple_of(at * 2 * half + half + column, 256)
                grad_x[level, :, pl.ds(first, 256)] = (factor * est_x[level, 0, :, place]).astype(BF16)
                grad_x[level, :, pl.ds(second, 256)] = (factor * est_x[level, 1, :, place]).astype(BF16)
                return carry

            lax.fori_loop(0, half // 256, gradients, 0)

    for step in range(0, NFFT, 256):
        windows[:, step : step + 256] = matmul_nt(grad_x[2], a2048[step : step + 256, :])
    for level, points in ((1, 1024), (0, 512)):
        count = NFFT // points
        stacked = jnp.concatenate(
            [grad_x[level, :, at * points : (at + 1) * points] for at in range(count)], axis=0
        )
        for step in range(0, points, 256):
            product = matmul_nt(stacked, analysis[level][step : step + 256, :])
            for at in range(count):
                first = at * (points // 4) + step
                windows[:, first : first + 256] = (
                    windows[:, first : first + 256] + product[at * ROWS : (at + 1) * ROWS]
                )

    grad_own[...] = overlap_add(windows[...]).reshape(LOCAL_CLIPS, 32, HOP)
    grad_copies = neighbours(grad_own, grad_tail, grad_head, grad_sem)
    for copy in grad_copies:
        copy.start()
    for copy in grad_copies:
        copy.wait_recv()
    write_windows(grad_win, joined(grad_own, grad_tail, grad_head))

    first_tile = me // 8 + 1

    def back_bins(step, carry):
        tile = lax.rem(first_tile + step, 8)
        product = matmul_nt(grad_win[...], syn[pl.ds(pl.multiple_of(tile * 256, 256), 256), :])
        for g in range(2):
            lanes = product[:, g * 128 : (g + 1) * 128]
            by_clip = [lanes[c * 32 : c * 32 + HOPS] for c in range(LOCAL_CLIPS)]
            for i, block in enumerate(swap_lane_groups(by_clip)):
                send_out[tile * 8 + g * 4 + i] = block.astype(BF16)
        for i in range(8):
            there = tile * 8 + i

            @pl.when(there != me)
            def _():
                pltpu.make_async_remote_copy(
                    src_ref=send_out.at[there],
                    dst_ref=recv_out.at[my_slot],
                    send_sem=out_send_sem,
                    recv_sem=out_recv_sem.at[my_chunk],
                    device_id=to_seg(there),
                    device_id_type=MESH,
                ).start()

            @pl.when(there == me)
            def _():
                pltpu.make_async_copy(
                    send_out.at[me], recv_out.at[my_slot], out_recv_sem.at[my_chunk]
                ).start()

        return carry

    lax.fori_loop(0, 8, back_bins, 0)

    seven = loss_recv.at[pl.ds(0, 2 * CLIP_GROUPS - 1)]
    pltpu.make_async_copy(seven, seven, loss_sem.at[1]).wait()
    loss_ref[...] = loss_recv[...].sum(axis=0) / (3 * CLIPS)

    for chunk in range(4):
        slabs = pl.ds(chunk * SLABS, SLABS)
        pltpu.make_async_copy(
            send_out.at[slabs], recv_out.at[slabs], out_recv_sem.at[chunk]
        ).wait()
        arrived = recv_out[slabs].astype(F32)
        one, two = halves(arrived[:8], arrived[8:])
        whole = jnp.concatenate([one[:, None], two[:, None]], axis=1)
        turned = whole.reshape(SLABS * HOPS, 128).T
        out_ref[:, chunk * 384 : (chunk + 1) * 384] = turned.astype(BF16)

    for copy in est_copies + grad_copies + (tgt_across,):
        copy.wait_send()

    @pl.when(jnp.logical_not(near_stays))
    def _():
        pltpu.make_async_copy(near_source, near_source, tgt_sem.at[2]).wait()

    for at, (source, there) in enumerate(heads):

        @pl.when((core == 0) & (there != me))
        def _(at=at):
            pltpu.make_async_copy(tgt_next, tgt_next, tgt_sem.at[3 + at]).wait()

    pltpu.make_async_copy(others, others, stat_sem.at[0]).wait()
    pltpu.make_async_copy(seven, seven, loss_sem.at[0]).wait()
    sent = pl.ds(0, SEGS - 1)
    pltpu.make_async_copy(send_in.at[sent], recv_in.at[sent], in_send_sem).wait()
    pltpu.make_async_copy(send_out.at[sent], recv_out.at[sent], out_send_sem).wait()


def body(spectra, target, lengths):
    vmem = pl.BlockSpec(memory_space=pltpu.VMEM)
    smem = pl.BlockSpec(memory_space=pltpu.SMEM)
    anywhere = pl.BlockSpec(memory_space=pl.ANY)
    slabs = pltpu.VMEM((SEGS, HOPS, 128), BF16)
    hops8 = pltpu.VMEM((2, 8, HOP), F32)
    hops24 = pltpu.VMEM((LOCAL_CLIPS, HOPS, HOP), BF16)
    hops32 = pltpu.VMEM((LOCAL_CLIPS, 32, HOP), F32)
    window = pltpu.VMEM((ROWS, NFFT), BF16)
    entries = pltpu.VMEM((3, ROWS, BINS), F32)
    dma = pltpu.SemaphoreType.DMA
    out, loss = pl.pallas_call(
        kernel,
        out_shape=(
            jax.ShapeDtypeStruct((ROWS, FRAMES), BF16),
            jax.ShapeDtypeStruct((1, 128), F32),
        ),
        in_specs=[vmem, vmem, smem] + [anywhere] * 4,
        out_specs=(vmem, vmem),
        scratch_shapes=[
            slabs, slabs, pltpu.VMEM((ROWS, 512), BF16), slabs, slabs,
            pltpu.VMEM((LOCAL_CLIPS, HOPS, HOP), F32), hops24, hops8,
            pltpu.VMEM((2048, 2048), BF16), pltpu.VMEM((512, 512), BF16),
            pltpu.VMEM((1024, 1024), BF16), pltpu.VMEM((2048, 2048), BF16),
            hops24, window, hops32, hops8, hops8, window,
            pltpu.VMEM((ROWS, NFFT), F32), entries, entries,
            pltpu.VMEM((3, 2, ROWS, BINS), F32), entries, entries,
            pltpu.VMEM((3, ROWS, NFFT), BF16),
            hops32, hops8, hops8, window,
            pltpu.VMEM((9, LOCAL_CLIPS, 8, 128), F32),
            pltpu.VMEM((1, 128), F32), pltpu.VMEM((WORKS, 1, 128), F32),
            pltpu.VMEM((1, 128), F32), pltpu.VMEM((2 * CLIP_GROUPS, 1, 128), F32),
            dma((4,)), dma, dma((4,)), dma, dma((4,)),
            dma((6,)), dma((4,)), dma((4,)), dma((2,)), dma((2,)),
        ],
        compiler_params=pltpu.CompilerParams(
            collective_id=0, has_side_effects=True, vmem_limit_bytes=60 * 2**20
        ),
        cost_estimate=pl.CostEstimate(
            flops=8 * 10**9, bytes_accessed=20 * 10**6, transcendentals=10**6
        ),
    )(
        spectra.reshape(ROWS, FRAMES),
        target,
        lengths,
        jnp.asarray(synthesis_table()),
        *(jnp.asarray(analysis_table(points)) for points in SIZES),
    )
    return loss[0, 0], out.reshape(LOCAL_CLIPS, 2, BINS // SEGS, FRAMES)


def solution(mesh):
    placed = (P("clip", None, "seg", None), P("clip", "seg"), P("clip"))
    return jax.shard_map(
        body,
        mesh=mesh,
        in_specs=placed,
        out_specs=(P(), P("clip", None, "seg", None)),
        check_vma=False,
    )
```

```python
import math

import jax
import jax.numpy as jnp
import ml_dtypes
import numpy as np
from jax import lax
from jax.experimental import pallas as pl
from jax.experimental.pallas import tpu as pltpu
from jax.sharding import PartitionSpec as P

BINS = 1024
NFFT = 2048
HOP = 512
FRAMES = 1536
CLIPS = 16
SEGS = 64
WORKS = 32
CLIP_GROUPS = 4
LOCAL_CLIPS = 4
HOPS = 24
ROWS = 128
SLABS = 16
EPS_MAG = 0.1
EPS_RATIO = 1e-05
SIZES = (512, 1024, 2048)
SCALE = float(FRAMES * BINS)
F32 = jnp.float32
BF16 = jnp.bfloat16
MESH = pl.DeviceIdType.MESH


def wave_table(bins_index, time_index, points, factor):
    halfway = points // 2
    is_sine = bins_index >= halfway
    harmonic = np.where(is_sine, bins_index - halfway, bins_index)
    angles = (harmonic * time_index % points).astype(np.float32) * np.float32(2.0 * math.pi / points)
    window = np.float32(0.5) - np.float32(0.5) * np.cos(
        time_index.astype(np.float32) * np.float32(2.0 * math.pi / points)
    )
    entry_value = np.where(is_sine, -np.sin(angles), np.cos(angles))
    return (entry_value * window * np.float32(factor)).astype(ml_dtypes.bfloat16)


def analysis_table(points):
    index = np.arange(points, dtype=np.int32)
    return wave_table(index[None, :], index[:, None], points, 1.0 / math.sqrt(points))


def synthesis_table():
    owner, part, bin_at = np.meshgrid(np.arange(64), np.arange(2), np.arange(16), indexing="ij")
    index = (part * BINS + owner * 16 + bin_at).reshape(-1).astype(np.int32)
    time = np.arange(NFFT, dtype=np.int32)
    return wave_table(index[:, None], time[None, :], NFFT, 1.0 / math.sqrt(BINS))


def to_seg(index):
    return {"seg": index}


def matmul(a, b):
    return lax.dot_general(a, b, (((1,), (0,)), ((), ())), preferred_element_type=F32)


def matmul_nt(a, b):
    return lax.dot_general(a, b, (((1,), (1,)), ((), ())), preferred_element_type=F32)


def swap_lane_groups(tiles):
    lane = lax.broadcasted_iota(jnp.int32, tiles[0].shape, 1) // 32
    results = []
    for j in range(4):
        result = tiles[j]
        for i in range(4):
            if i != j:
                moved = pltpu.roll(tiles[i], (32 * (i - j)) % 128, 1)
                result = jnp.where(lane == i, moved, result)
        results.append(result)
    return results


def overlap_add(windows_ref, quarters=4):
    total = windows_ref[:, :HOP]
    for q in range(1, quarters):
        total = total + pltpu.roll(windows_ref[:, q * HOP : (q + 1) * HOP], q, 0)
    return total


def write_windows(windows_ref, wave):
    windows_ref[:, :HOP] = wave.astype(BF16)
    for q in range(1, 4):
        windows_ref[:, q * HOP : (q + 1) * HOP] = pltpu.roll(wave, ROWS - q, 0).astype(BF16)


def halves(first, second):
    shape = first.shape
    first, second = first.reshape(-1, 128), second.reshape(-1, 128)
    low = lax.broadcasted_iota(jnp.int32, first.shape, 1) < 64
    one = jnp.where(low, first, pltpu.roll(second, 64, 1))
    other = jnp.where(low, pltpu.roll(first, 64, 1), second)
    return one.reshape(shape), other.reshape(shape)


def fold_rows(tile):
    by_clip = tile.reshape(LOCAL_CLIPS, 4, 8, tile.shape[1]).sum(axis=1)
    return by_clip[:, :, :128] + by_clip[:, :, 128:]


def kernel(
    spec_ref, target_ref, lengths_ref, syn_hbm, a512_hbm, a1024_hbm, a2048_hbm,
    out_ref, loss_ref,
    send_in, recv_in, chunk_in, send_out, recv_out, tgt_rows, tgt_raw, tgt_next,
    syn, a512, a1024, a2048,
    tgt, tgt_win, est_own, est_tail, est_head, est_win,
    windows, mag_windows, tgt_mag, tgt_log, grad_x,
    grad_own, tail_send, head_send, grad_tail, grad_head, grad_win,
    sums, stat_send, stat_recv, loss_send, loss_recv,
    table_sem, in_send_sem, in_recv_sem, out_send_sem, out_recv_sem,
    tgt_sem, est_sem, grad_sem, stat_sem, loss_sem,
):
    me = lax.axis_index("seg")
    clip = lax.axis_index("clip")
    analysis = (a512, a1024, a2048)
    spot = me // 4
    core = lax.rem(me, 2)
    side = lax.rem(me // 2, 2)
    work = spot * 2 + core

    def device_of(work_index, side_index):
        return (work_index // 2) * 4 + side_index * 2 + lax.rem(work_index, 2)

    def slot_of(work_index, side_index):
        return (work_index // 8) * 16 + side_index * 8 + lax.rem(work_index, 8)

    after = device_of(lax.rem(work + 1, WORKS), side)
    before = device_of(lax.rem(work + WORKS - 1, WORKS), side)
    my_slot = slot_of(work, side)
    loss_peers = [
        (lax.rem(clip + step // 2, CLIP_GROUPS), device_of(work, lax.rem(side + step, 2)))
        for step in range(1, 2 * CLIP_GROUPS)
    ]

    barrier = pltpu.get_barrier_semaphore()

    def greet(step, carry):
        pl.semaphore_signal(
            barrier, inc=1, device_id=to_seg(lax.rem(me + step, SEGS)), device_id_type=MESH
        )
        return carry

    lax.fori_loop(1, SEGS, greet, 0)
    for peer in loss_peers[1:]:
        pl.semaphore_signal(barrier, inc=1, device_id=peer, device_id_type=MESH)

    table_copies = [
        pltpu.make_async_copy(source, held, table_sem.at[at])
        for at, (source, held) in enumerate(
            ((a512_hbm, a512), (a1024_hbm, a1024), (a2048_hbm, a2048), (syn_hbm, syn))
        )
    ]
    for copy in table_copies:
        copy.start()

    for hop in range(HOPS):
        tgt_rows[:, hop, :] = target_ref[:, hop * HOP : (hop + 1) * HOP].astype(F32)
    tgt_raw[...] = tgt_rows[...].astype(BF16)
    for part in range(4):
        turned = spec_ref[:, 384 * part : 384 * (part + 1)].astype(F32).T
        turned = turned.reshape(8, 2, HOPS, 128)
        for at, message in enumerate(halves(turned[:, 0], turned[:, 1])):
            first = part * 16 + at * 8
            send_in[first : first + 8] = message.astype(BF16)

    pl.semaphore_wait(barrier, SEGS - 1 + len(loss_peers) - 1)

    def hold(to_side):
        return tgt_raw.at[pl.ds(2 * to_side, 2)], tgt.at[pl.ds(2 * core, 2)]

    across_source, across_place = hold(1 - side)
    tgt_across = pltpu.make_async_remote_copy(
        src_ref=across_source,
        dst_ref=across_place,
        send_sem=tgt_sem.at[0],
        recv_sem=tgt_sem.at[1],
        device_id=to_seg(spot * 4 + (1 - side) * 2 + side),
        device_id_type=MESH,
    )
    tgt_across.start()
    near_source, near_place = hold(side)
    near_stays = core == side

    @pl.when(near_stays)
    def _():
        pltpu.make_async_copy(near_source, near_place, tgt_sem.at[1]).start()

    @pl.when(jnp.logical_not(near_stays))
    def _():
        pltpu.make_async_remote_copy(
            src_ref=near_source,
            dst_ref=near_place,
            send_sem=tgt_sem.at[2],
            recv_sem=tgt_sem.at[1],
            device_id=to_seg(spot * 4 + side * 3),
            device_id_type=MESH,
        ).start()

    ahead = lax.rem(spot * 2 + side + WORKS - 1, WORKS)
    heads = [
        (tgt_rows.at[pl.ds(2 * to_side, 2), pl.ds(0, 8), :], device_of(ahead, to_side))
        for to_side in range(2)
    ]
    for at, (source, there) in enumerate(heads):

        @pl.when((core == 0) & (there != me))
        def _(at=at, source=source, there=there):
            pltpu.make_async_remote_copy(
                src_ref=source,
                dst_ref=tgt_next,
                send_sem=tgt_sem.at[3 + at],
                recv_sem=tgt_sem.at[5],
                device_id=to_seg(there),
                device_id_type=MESH,
            ).start()

        @pl.when((core == 0) & (there == me))
        def _(source=source):
            pltpu.make_async_copy(source, tgt_next, tgt_sem.at[5]).start()

    my_chunk = me // SLABS

    def send_bins(step, carry):
        there = lax.rem(me + step, SEGS)
        pltpu.make_async_remote_copy(
            src_ref=send_in.at[
                slot_of((there // 4) * 2 + lax.rem(there, 2), lax.rem(there // 2, 2))
            ],
            dst_ref=recv_in.at[me],
            send_sem=in_send_sem,
            recv_sem=in_recv_sem.at[my_chunk],
            device_id=to_seg(there),
            device_id_type=MESH,
        ).start()
        return carry

    lax.fori_loop(1, SEGS, send_bins, 0)
    pltpu.make_async_copy(send_in.at[my_slot], recv_in.at[me], in_recv_sem.at[my_chunk]).start()

    row = lax.broadcasted_iota(jnp.int32, (ROWS, 1), 0)
    row_clip = row // 32
    row_hop = lax.rem(row, 32)
    row_length = jnp.where(
        lax.rem(row_clip, 2) == 0, lengths_ref[2 * side], lengths_ref[2 * side + 1]
    )
    inside = work * (2 * HOPS) + (row_clip // 2) * HOPS + row_hop < row_length
    usable = inside & (row_hop < HOPS)
    log_weight = (2.0 * SCALE) / (row_length * BINS).astype(F32)
    for level in range(2):
        mag_windows[level] = jnp.zeros((ROWS, NFFT), F32)

    pltpu.make_async_copy(tgt_raw, tgt, tgt_sem.at[1]).wait()
    pltpu.make_async_copy(tgt_next, tgt_next, tgt_sem.at[5]).wait()
    own = tgt[...].astype(F32)
    first_half = jnp.concatenate([own[:2], own[2:, :8]], axis=1)
    second_half = jnp.concatenate([own[2:], tgt_next[...]], axis=1)
    own = jnp.concatenate([first_half, second_half], axis=0).reshape(ROWS, HOP)
    write_windows(tgt_win, jnp.where(inside, own, 0.0))

    def frames_of(windows_ref, points):
        stride = points // 4
        parts = [
            windows_ref[:, at * stride : at * stride + points] for at in range(HOP // stride)
        ]
        return parts[0] if len(parts) == 1 else jnp.concatenate(parts, axis=0)

    for level, points in enumerate(SIZES):
        half = points // 2
        count = NFFT // points
        table_copies[level].wait()

        def target_columns(step, energy, level=level, points=points, half=half, count=count):
            column = pl.multiple_of(step * 256, 256)
            frames = frames_of(tgt_win, points)
            real = matmul(frames, analysis[level][:, pl.ds(column, 256)])
            imag = matmul(frames, analysis[level][:, pl.ds(half + column, 256)])
            power = real * real + imag * imag + EPS_MAG
            for at in range(count):
                place = pl.ds(pl.multiple_of(at * half + column, 256), 256)
                part = power[at * ROWS : (at + 1) * ROWS]
                tgt_mag[level, :, place] = jnp.sqrt(part)
                tgt_log[level, :, place] = 0.5 * jnp.log(part)
                energy = energy + fold_rows(jnp.where(usable, part, 0.0))
            return energy

        start = jnp.zeros((LOCAL_CLIPS, 8, 128), F32)
        sums[3 + level] = lax.fori_loop(0, half // 256, target_columns, start)

    table_copies[3].wait()
    for turn in range(4):
        chunk = lax.rem(my_chunk + (4 - turn), 4)
        slabs = pl.ds(pl.multiple_of(chunk * SLABS, SLABS), SLABS)
        pltpu.make_async_copy(
            send_in.at[slabs], recv_in.at[slabs], in_recv_sem.at[chunk]
        ).wait()
        arrived = recv_in[slabs].astype(F32).reshape(4, 4, HOPS, 128)
        by_source = [arrived[:, i].reshape(4 * HOPS, 128) for i in range(4)]
        by_clip = swap_lane_groups(by_source)
        for c in range(LOCAL_CLIPS):
            for g in range(4):
                block = by_clip[c][g * HOPS : (g + 1) * HOPS]
                block = jnp.concatenate([block, jnp.zeros((8, 128), F32)], axis=0)
                chunk_in[c * 32 : (c + 1) * 32, g * 128 : (g + 1) * 128] = block.astype(BF16)
        for tile in range(4):
            columns = slice(tile * 512, (tile + 1) * 512)
            product = matmul(
                chunk_in[...], syn[pl.ds(pl.multiple_of(chunk * 512, 512), 512), columns]
            )
            if turn == 0:
                windows[:, columns] = product
            else:
                windows[:, columns] = windows[:, columns] + product

    def neighbours(tail_source, tail, head_source, head, sem):
        return (
            pltpu.make_async_remote_copy(
                src_ref=tail_source,
                dst_ref=tail,
                send_sem=sem.at[0],
                recv_sem=sem.at[1],
                device_id=to_seg(after),
                device_id_type=MESH,
            ),
            pltpu.make_async_remote_copy(
                src_ref=head_source,
                dst_ref=head,
                send_sem=sem.at[2],
                recv_sem=sem.at[3],
                device_id=to_seg(before),
                device_id_type=MESH,
            ),
        )

    def joined(own, tail, head):
        before_us = jnp.where(work == 0, 0.0, tail)
        hop = lax.broadcasted_iota(jnp.int32, head.shape, 1)
        after_us = jnp.where(hop < 3, head, 0.0)
        one, two = own[:2], own[2:]
        spill = one[:, HOPS:]
        middle = jnp.where(hop < 3, spill + two[:, :8], 0.0)
        one = jnp.concatenate([one[:, :8] + before_us, one[:, 8:HOPS], middle], axis=1)
        two = jnp.concatenate(
            [two[:, :8] + spill, two[:, 8:HOPS], two[:, HOPS:] + after_us], axis=1
        )
        whole = jnp.concatenate([one, two], axis=0)
        return jnp.where(inside, whole.reshape(ROWS, HOP), 0.0)

    est_own[...] = overlap_add(windows).reshape(LOCAL_CLIPS, 32, HOP)
    est_copies = neighbours(
        est_own.at[pl.ds(2, 2), pl.ds(HOPS, 8), :],
        est_tail,
        est_own.at[pl.ds(0, 2), pl.ds(0, 8), :],
        est_head,
        est_sem,
    )
    for copy in est_copies:
        copy.start()
    for copy in est_copies:
        copy.wait_recv()
    write_windows(est_win, joined(est_own[...], est_tail[...], est_head[...]))

    for level, points in enumerate(SIZES):
        half = points // 2
        count = NFFT // points
        spread = jnp.zeros((LOCAL_CLIPS, 8, 128), F32)
        logterm = jnp.zeros((LOCAL_CLIPS, 8, 128), F32)
        for column in range(0, half, 256):
            frames = frames_of(est_win, points)
            all_real = matmul(frames, analysis[level][:, column : column + 256])
            all_imag = matmul(frames, analysis[level][:, half + column : half + column + 256])
            for at in range(count):
                rows = slice(at * ROWS, (at + 1) * ROWS)
                real, imag = all_real[rows], all_imag[rows]
                power = real * real + imag * imag + EPS_MAG
                inverse = lax.rsqrt(power)
                place = slice(at * half + column, at * half + column + 256)
                gap = power * inverse - tgt_mag[level, :, place]
                log_gap = 0.5 * jnp.log(power) - tgt_log[level, :, place]
                mag_factor = jnp.where(usable, gap * inverse, 0.0)
                log_factor = jnp.where(usable, log_gap * inverse * inverse * log_weight, 0.0)
                for part, first in (
                    (real, at * points + column),
                    (imag, at * points + half + column),
                ):
                    lanes = slice(first, first + 256)
                    grad_x[level, :ROWS, lanes] = (mag_factor * part).astype(BF16)
                    grad_x[level, ROWS:, lanes] = (log_factor * part).astype(BF16)
                spread = spread + fold_rows(jnp.where(usable, gap * gap, 0.0))
                logterm = logterm + fold_rows(jnp.where(usable, log_gap * log_gap, 0.0))
        sums[level] = spread
        sums[6 + level] = logterm

    flat = sums[...].reshape(36, 8, 128).sum(axis=1)
    flat = jnp.sum(flat, axis=1, keepdims=True)
    lane = lax.broadcasted_iota(jnp.int32, (36, 128), 1)
    line = lax.broadcasted_iota(jnp.int32, (36, 128), 0)
    own_stats = jnp.sum(jnp.where(lane == line, flat, 0.0), axis=0, keepdims=True)
    stat_send[...] = own_stats
    stat_recv[work] = own_stats

    def send_stats(step, carry):
        pltpu.make_async_remote_copy(
            src_ref=stat_send,
            dst_ref=stat_recv.at[work],
            send_sem=stat_sem.at[0],
            recv_sem=stat_sem.at[1],
            device_id=to_seg(device_of(lax.rem(work + step, WORKS), side)),
            device_id_type=MESH,
        ).start()
        return carry

    lax.fori_loop(1, WORKS, send_stats, 0)
    def add_to(ref, first, product):
        ref[:, first : first + 256] = ref[:, first : first + 256] + product

    for step in range(0, NFFT, 256):
        product = matmul_nt(grad_x[2], a2048[step : step + 256, :])
        mag_windows[2, :, step : step + 256] = product[:ROWS]
        windows[:, step : step + 256] = product[ROWS:]
    for level, points in ((1, 1024), (0, 512)):
        count = NFFT // points
        stacked = jnp.concatenate(
            [grad_x[level, :, at * points : (at + 1) * points] for at in range(count)], axis=0
        )
        for step in range(0, points, 256):
            product = matmul_nt(stacked, analysis[level][step : step + 256, :])
            for at in range(count):
                first = at * (points // 4) + step
                base = at * 2 * ROWS
                add_to(mag_windows.at[level], first, product[base : base + ROWS])
                add_to(windows, first, product[base + ROWS : base + 2 * ROWS])

    for level in range(3):
        grad_own[level] = overlap_add(mag_windows.at[level], level + 2)
    grad_own[3] = overlap_add(windows)
    hop8 = lax.broadcasted_iota(jnp.int32, (2, 8, HOP), 1)
    for pair in range(2):
        upper = grad_own[2 * pair].reshape(LOCAL_CLIPS, 32, HOP)
        lower = grad_own[2 * pair + 1].reshape(LOCAL_CLIPS, 32, HOP)
        tail_send[pair] = jnp.where(
            hop8 < 4, upper[2:, HOPS:], pltpu.roll(lower[2:, HOPS:], 4, 1)
        )
        head_send[pair] = jnp.where(hop8 < 4, upper[:2, :8], pltpu.roll(lower[:2, :8], 4, 1))
    grad_copies = neighbours(tail_send, grad_tail, head_send, grad_head, grad_sem)
    for copy in grad_copies:
        copy.start()

    others = stat_recv.at[pl.ds(0, WORKS - 1)]
    pltpu.make_async_copy(others, others, stat_sem.at[1]).wait()
    totals = stat_recv[...].sum(axis=0)

    place = lax.broadcasted_iota(jnp.int32, (1, 128), 1)
    low_half = lax.rem(place, 4) < 2
    totals = totals + jnp.where(low_half, pltpu.roll(totals, 126, 1), pltpu.roll(totals, 2, 1))
    energy = pltpu.roll(totals, 128 - 12, 1)
    logterm = pltpu.roll(totals, 128 - 24, 1)
    filled = place < 12
    lane_length = jnp.where(
        lax.rem(place, 2) == 0, lengths_ref[2 * side], lengths_ref[2 * side + 1]
    )
    entries = (lane_length * BINS).astype(F32)
    safe_energy = jnp.where(filled, energy, 1.0)
    safe_spread = jnp.where(filled, totals, 1.0) + EPS_RATIO
    terms = jnp.where(filled & low_half, jnp.sqrt(safe_spread / safe_energy) + logterm / entries, 0.0)
    weights = SCALE / jnp.sqrt(safe_spread * safe_energy)
    weights = jnp.broadcast_to(weights, (ROWS, 128))
    pick_lane = lax.broadcasted_iota(jnp.int32, (ROWS, 128), 1)
    pick_row = lax.broadcasted_iota(jnp.int32, (ROWS, 128), 0) // 32
    mag_weights = [
        jnp.sum(jnp.where(pick_lane == level * 4 + pick_row, weights, 0.0), axis=1, keepdims=True)
        for level in range(3)
    ]
    own = grad_own[3]
    for level in range(3):
        own = own + mag_weights[level] * grad_own[level]
    for copy in grad_copies:
        copy.wait_recv()

    def weighted(received):
        def row_of(component):
            block = received[component // 2]
            return block if component % 2 == 0 else pltpu.roll(block, 4, 1)

        total = row_of(3)
        for level in range(3):
            weight = mag_weights[level].reshape(LOCAL_CLIPS, 32, 1)[:2, :8]
            total = total + weight * row_of(level)
        return jnp.where(hop8 < 3, total, 0.0)

    write_windows(
        grad_win,
        joined(own.reshape(LOCAL_CLIPS, 32, HOP), weighted(grad_tail), weighted(grad_head)),
    )

    first_tile = me // 8 + 1

    def back_bins(step, carry):
        tile = lax.rem(first_tile + step, 8)
        product = matmul_nt(grad_win[...], syn[pl.ds(pl.multiple_of(tile * 256, 256), 256), :])
        for g in range(2):
            lanes = product[:, g * 128 : (g + 1) * 128]
            by_clip = [lanes[c * 32 : c * 32 + HOPS] for c in range(LOCAL_CLIPS)]
            for i, block in enumerate(swap_lane_groups(by_clip)):
                send_out[tile * 8 + g * 4 + i] = block.astype(BF16)
        for i in range(8):
            there = tile * 8 + i

            @pl.when(there != me)
            def _():
                pltpu.make_async_remote_copy(
                    src_ref=send_out.at[there],
                    dst_ref=recv_out.at[my_slot],
                    send_sem=out_send_sem,
                    recv_sem=out_recv_sem.at[my_chunk],
                    device_id=to_seg(there),
                    device_id_type=MESH,
                ).start()

            @pl.when(there == me)
            def _():
                pltpu.make_async_copy(
                    send_out.at[me], recv_out.at[my_slot], out_recv_sem.at[my_chunk]
                ).start()

        return carry

    lax.fori_loop(0, 8, back_bins, 0)

    own_loss = jnp.sum(terms, axis=1, keepdims=True) + jnp.zeros((1, 128), F32)
    loss_send[...] = own_loss
    my_loss = clip * 2 + side
    loss_recv[my_loss] = own_loss
    for peer in loss_peers:
        pltpu.make_async_remote_copy(
            src_ref=loss_send,
            dst_ref=loss_recv.at[my_loss],
            send_sem=loss_sem.at[0],
            recv_sem=loss_sem.at[1],
            device_id=peer,
            device_id_type=MESH,
        ).start()

    seven = loss_recv.at[pl.ds(0, 2 * CLIP_GROUPS - 1)]
    pltpu.make_async_copy(seven, seven, loss_sem.at[1]).wait()
    loss_ref[...] = loss_recv[...].sum(axis=0) / (3 * CLIPS)

    for chunk in range(4):
        slabs = pl.ds(chunk * SLABS, SLABS)
        pltpu.make_async_copy(
            send_out.at[slabs], recv_out.at[slabs], out_recv_sem.at[chunk]
        ).wait()
        arrived = recv_out[slabs].astype(F32)
        one, two = halves(arrived[:8], arrived[8:])
        whole = jnp.concatenate([one[:, None], two[:, None]], axis=1)
        turned = whole.reshape(SLABS * HOPS, 128).T
        out_ref[:, chunk * 384 : (chunk + 1) * 384] = turned.astype(BF16)

    for copy in est_copies + grad_copies + (tgt_across,):
        copy.wait_send()

    @pl.when(jnp.logical_not(near_stays))
    def _():
        pltpu.make_async_copy(near_source, near_source, tgt_sem.at[2]).wait()

    for at, (source, there) in enumerate(heads):

        @pl.when((core == 0) & (there != me))
        def _(at=at):
            pltpu.make_async_copy(tgt_next, tgt_next, tgt_sem.at[3 + at]).wait()

    pltpu.make_async_copy(others, others, stat_sem.at[0]).wait()
    pltpu.make_async_copy(seven, seven, loss_sem.at[0]).wait()
    sent = pl.ds(0, SEGS - 1)
    pltpu.make_async_copy(send_in.at[sent], recv_in.at[sent], in_send_sem).wait()
    pltpu.make_async_copy(send_out.at[sent], recv_out.at[sent], out_send_sem).wait()


def body(spectra, target, lengths):
    vmem = pl.BlockSpec(memory_space=pltpu.VMEM)
    smem = pl.BlockSpec(memory_space=pltpu.SMEM)
    anywhere = pl.BlockSpec(memory_space=pl.ANY)
    slabs = pltpu.VMEM((SEGS, HOPS, 128), BF16)
    pairs = pltpu.VMEM((2, 2, 8, HOP), F32)
    hops8 = pltpu.VMEM((2, 8, HOP), F32)
    hops24 = pltpu.VMEM((LOCAL_CLIPS, HOPS, HOP), BF16)
    hops32 = pltpu.VMEM((LOCAL_CLIPS, 32, HOP), F32)
    window = pltpu.VMEM((ROWS, NFFT), BF16)
    entries = pltpu.VMEM((3, ROWS, BINS), F32)
    dma = pltpu.SemaphoreType.DMA
    out, loss = pl.pallas_call(
        kernel,
        out_shape=(
            jax.ShapeDtypeStruct((ROWS, FRAMES), BF16),
            jax.ShapeDtypeStruct((1, 128), F32),
        ),
        in_specs=[vmem, vmem, smem] + [anywhere] * 4,
        out_specs=(vmem, vmem),
        scratch_shapes=[
            slabs, slabs, pltpu.VMEM((ROWS, 512), BF16), slabs, slabs,
            pltpu.VMEM((LOCAL_CLIPS, HOPS, HOP), F32), hops24, hops8,
            pltpu.VMEM((2048, 2048), BF16), pltpu.VMEM((512, 512), BF16),
            pltpu.VMEM((1024, 1024), BF16), pltpu.VMEM((2048, 2048), BF16),
            hops24, window, hops32, hops8, hops8, window,
            pltpu.VMEM((ROWS, NFFT), F32), pltpu.VMEM((3, ROWS, NFFT), F32), entries, entries,
            pltpu.VMEM((3, 2 * ROWS, NFFT), BF16),
            pltpu.VMEM((4, ROWS, HOP), F32), pairs, pairs, pairs, pairs, window,
            pltpu.VMEM((9, LOCAL_CLIPS, 8, 128), F32),
            pltpu.VMEM((1, 128), F32), pltpu.VMEM((WORKS, 1, 128), F32),
            pltpu.VMEM((1, 128), F32), pltpu.VMEM((2 * CLIP_GROUPS, 1, 128), F32),
            dma((4,)), dma, dma((4,)), dma, dma((4,)),
            dma((6,)), dma((4,)), dma((4,)), dma((2,)), dma((2,)),
        ],
        compiler_params=pltpu.CompilerParams(
            collective_id=0, has_side_effects=True, vmem_limit_bytes=60 * 2**20
        ),
        cost_estimate=pl.CostEstimate(
            flops=8 * 10**9, bytes_accessed=20 * 10**6, transcendentals=10**6
        ),
    )(
        spectra.reshape(ROWS, FRAMES),
        target,
        lengths,
        jnp.asarray(synthesis_table()),
        *(jnp.asarray(analysis_table(points)) for points in SIZES),
    )
    return loss[0, 0], out.reshape(LOCAL_CLIPS, 2, BINS // SEGS, FRAMES)


def solution(mesh):
    placed = (P("clip", None, "seg", None), P("clip", "seg"), P("clip"))
    return jax.shard_map(
        body,
        mesh=mesh,
        in_specs=placed,
        out_specs=(P(), P("clip", None, "seg", None)),
        check_vma=False,
    )
```

```python
import math

import jax
import jax.numpy as jnp
import ml_dtypes
import numpy as np
from jax import lax
from jax.experimental import pallas as pl
from jax.experimental.pallas import tpu as pltpu
from jax.sharding import PartitionSpec as P

BINS = 1024
NFFT = 2048
HOP = 512
FRAMES = 1536
CLIPS = 16
SEGS = 64
WORKS = 32
CLIP_GROUPS = 4
LOCAL_CLIPS = 4
HOPS = 24
ROWS = 128
SLABS = 16
EPS_MAG = 0.1
EPS_RATIO = 1e-05
SIZES = (512, 1024, 2048)
SCALE = float(FRAMES * BINS)
F32 = jnp.float32
BF16 = jnp.bfloat16
MESH = pl.DeviceIdType.MESH


def wave_table(bins_index, time_index, points, factor):
    halfway = points // 2
    is_sine = bins_index >= halfway
    harmonic = np.where(is_sine, bins_index - halfway, bins_index)
    angles = (harmonic * time_index % points).astype(np.float32) * np.float32(2.0 * math.pi / points)
    window = np.float32(0.5) - np.float32(0.5) * np.cos(
        time_index.astype(np.float32) * np.float32(2.0 * math.pi / points)
    )
    entry_value = np.where(is_sine, -np.sin(angles), np.cos(angles))
    return (entry_value * window * np.float32(factor)).astype(ml_dtypes.bfloat16)


def analysis_table(points):
    index = np.arange(points, dtype=np.int32)
    return wave_table(index[None, :], index[:, None], points, 1.0 / math.sqrt(points))


def synthesis_table():
    owner, part, bin_at = np.meshgrid(np.arange(64), np.arange(2), np.arange(16), indexing="ij")
    index = (part * BINS + owner * 16 + bin_at).reshape(-1).astype(np.int32)
    time = np.arange(NFFT, dtype=np.int32)
    return wave_table(index[:, None], time[None, :], NFFT, 1.0 / math.sqrt(BINS))


def to_seg(index):
    return {"seg": index}


def matmul(a, b):
    return lax.dot_general(a, b, (((1,), (0,)), ((), ())), preferred_element_type=F32)


def matmul_nt(a, b):
    return lax.dot_general(a, b, (((1,), (1,)), ((), ())), preferred_element_type=F32)


def swap_lane_groups(tiles):
    lane = lax.broadcasted_iota(jnp.int32, tiles[0].shape, 1) // 32
    results = []
    for j in range(4):
        result = tiles[j]
        for i in range(4):
            if i != j:
                moved = pltpu.roll(tiles[i], (32 * (i - j)) % 128, 1)
                result = jnp.where(lane == i, moved, result)
        results.append(result)
    return results


def overlap_add(windows_ref, quarters=4):
    total = windows_ref[:, :HOP]
    for q in range(1, quarters):
        total = total + pltpu.roll(windows_ref[:, q * HOP : (q + 1) * HOP], q, 0)
    return total


def write_windows(windows_ref, wave):
    windows_ref[:, :HOP] = wave.astype(BF16)
    for q in range(1, 4):
        windows_ref[:, q * HOP : (q + 1) * HOP] = pltpu.roll(wave, ROWS - q, 0).astype(BF16)


def halves(first, second):
    shape = first.shape
    first, second = first.reshape(-1, 128), second.reshape(-1, 128)
    low = lax.broadcasted_iota(jnp.int32, first.shape, 1) < 64
    one = jnp.where(low, first, pltpu.roll(second, 64, 1))
    other = jnp.where(low, pltpu.roll(first, 64, 1), second)
    return one.reshape(shape), other.reshape(shape)


def fold_rows(tile):
    by_clip = tile.reshape(LOCAL_CLIPS, 4, 8, tile.shape[1]).sum(axis=1)
    return by_clip[:, :, :128] + by_clip[:, :, 128:]


def kernel(
    spec_ref, target_ref, lengths_ref, syn_hbm, a512_hbm, a1024_hbm, a2048_hbm,
    out_ref, loss_ref,
    send_in, recv_in, chunk_in, send_out, recv_out, tgt_rows, tgt_raw, tgt_next,
    syn, a512, a1024, a2048,
    tgt, tgt_win, est_own, est_tail, est_head, est_win,
    windows, mag_windows, tgt_mag, tgt_log, grad_x,
    grad_own, tail_send, head_send, grad_tail, grad_head, grad_win,
    sums, stat_send, stat_recv, loss_send, loss_recv,
    table_sem, in_send_sem, in_recv_sem, out_send_sem, out_recv_sem,
    tgt_sem, est_sem, grad_sem, stat_sem, loss_sem,
):
    me = lax.axis_index("seg")
    clip = lax.axis_index("clip")
    analysis = (a512, a1024, a2048)
    spot = me // 4
    core = lax.rem(me, 2)
    side = lax.rem(me // 2, 2)
    work = spot * 2 + core

    def device_of(work_index, side_index):
        return (work_index // 2) * 4 + side_index * 2 + lax.rem(work_index, 2)

    def slot_of(work_index, side_index):
        return (work_index // 8) * 16 + side_index * 8 + lax.rem(work_index, 8)

    after = device_of(lax.rem(work + 1, WORKS), side)
    before = device_of(lax.rem(work + WORKS - 1, WORKS), side)
    my_slot = slot_of(work, side)
    loss_peers = [
        (lax.rem(clip + step // 2, CLIP_GROUPS), device_of(work, lax.rem(side + step, 2)))
        for step in range(1, 2 * CLIP_GROUPS)
    ]

    barrier = pltpu.get_barrier_semaphore()

    def greet(step, carry):
        pl.semaphore_signal(
            barrier, inc=1, device_id=to_seg(lax.rem(me + step, SEGS)), device_id_type=MESH
        )
        return carry

    lax.fori_loop(1, SEGS, greet, 0)
    for peer in loss_peers[1:]:
        pl.semaphore_signal(barrier, inc=1, device_id=peer, device_id_type=MESH)

    table_copies = [
        pltpu.make_async_copy(source, held, table_sem.at[at])
        for at, (source, held) in enumerate(
            ((a512_hbm, a512), (a1024_hbm, a1024), (a2048_hbm, a2048), (syn_hbm, syn))
        )
    ]
    for copy in table_copies:
        copy.start()

    for hop in range(HOPS):
        tgt_rows[:, hop, :] = target_ref[:, hop * HOP : (hop + 1) * HOP].astype(F32)
    tgt_raw[...] = tgt_rows[...].astype(BF16)
    for part in range(4):
        turned = spec_ref[:, 384 * part : 384 * (part + 1)].astype(F32).T
        turned = turned.reshape(8, 2, HOPS, 128)
        for at, message in enumerate(halves(turned[:, 0], turned[:, 1])):
            first = part * 16 + at * 8
            send_in[first : first + 8] = message.astype(BF16)

    pl.semaphore_wait(barrier, SEGS - 1 + len(loss_peers) - 1)

    my_chunk = me // SLABS

    def send_bins(step, carry):
        there = lax.rem(me + step, SEGS)
        pltpu.make_async_remote_copy(
            src_ref=send_in.at[
                slot_of((there // 4) * 2 + lax.rem(there, 2), lax.rem(there // 2, 2))
            ],
            dst_ref=recv_in.at[me],
            send_sem=in_send_sem,
            recv_sem=in_recv_sem.at[my_chunk],
            device_id=to_seg(there),
            device_id_type=MESH,
        ).start()
        return carry

    lax.fori_loop(1, SEGS, send_bins, 0)
    pltpu.make_async_copy(send_in.at[my_slot], recv_in.at[me], in_recv_sem.at[my_chunk]).start()

    def hold(to_side):
        return tgt_raw.at[pl.ds(2 * to_side, 2)], tgt.at[pl.ds(2 * core, 2)]

    across_source, across_place = hold(1 - side)
    tgt_across = pltpu.make_async_remote_copy(
        src_ref=across_source,
        dst_ref=across_place,
        send_sem=tgt_sem.at[0],
        recv_sem=tgt_sem.at[1],
        device_id=to_seg(spot * 4 + (1 - side) * 2 + side),
        device_id_type=MESH,
    )
    tgt_across.start()
    near_source, near_place = hold(side)
    near_stays = core == side

    @pl.when(near_stays)
    def _():
        pltpu.make_async_copy(near_source, near_place, tgt_sem.at[1]).start()

    @pl.when(jnp.logical_not(near_stays))
    def _():
        pltpu.make_async_remote_copy(
            src_ref=near_source,
            dst_ref=near_place,
            send_sem=tgt_sem.at[2],
            recv_sem=tgt_sem.at[1],
            device_id=to_seg(spot * 4 + side * 3),
            device_id_type=MESH,
        ).start()

    ahead = lax.rem(spot * 2 + side + WORKS - 1, WORKS)
    heads = [
        (tgt_rows.at[pl.ds(2 * to_side, 2), pl.ds(0, 8), :], device_of(ahead, to_side))
        for to_side in range(2)
    ]
    for at, (source, there) in enumerate(heads):

        @pl.when((core == 0) & (there != me))
        def _(at=at, source=source, there=there):
            pltpu.make_async_remote_copy(
                src_ref=source,
                dst_ref=tgt_next,
                send_sem=tgt_sem.at[3 + at],
                recv_sem=tgt_sem.at[5],
                device_id=to_seg(there),
                device_id_type=MESH,
            ).start()

        @pl.when((core == 0) & (there == me))
        def _(source=source):
            pltpu.make_async_copy(source, tgt_next, tgt_sem.at[5]).start()

    row = lax.broadcasted_iota(jnp.int32, (ROWS, 1), 0)
    row_clip = row // 32
    row_hop = lax.rem(row, 32)
    row_length = jnp.where(
        lax.rem(row_clip, 2) == 0, lengths_ref[2 * side], lengths_ref[2 * side + 1]
    )
    inside = work * (2 * HOPS) + (row_clip // 2) * HOPS + row_hop < row_length
    usable = inside & (row_hop < HOPS)
    log_weight = (2.0 * SCALE) / (row_length * BINS).astype(F32)
    for level in range(2):
        mag_windows[level] = jnp.zeros((ROWS, NFFT), F32)

    table_copies[3].wait()
    for turn in range(4):
        chunk = lax.rem(my_chunk + (3 - turn), 4)
        slabs = pl.ds(pl.multiple_of(chunk * SLABS, SLABS), SLABS)
        pltpu.make_async_copy(
            send_in.at[slabs], recv_in.at[slabs], in_recv_sem.at[chunk]
        ).wait()
        arrived = recv_in[slabs].astype(F32).reshape(4, 4, HOPS, 128)
        by_source = [arrived[:, i].reshape(4 * HOPS, 128) for i in range(4)]
        by_clip = swap_lane_groups(by_source)
        for c in range(LOCAL_CLIPS):
            for g in range(4):
                block = by_clip[c][g * HOPS : (g + 1) * HOPS]
                block = jnp.concatenate([block, jnp.zeros((8, 128), F32)], axis=0)
                chunk_in[c * 32 : (c + 1) * 32, g * 128 : (g + 1) * 128] = block.astype(BF16)
        for tile in range(4):
            columns = slice(tile * 512, (tile + 1) * 512)
            product = matmul(
                chunk_in[...], syn[pl.ds(pl.multiple_of(chunk * 512, 512), 512), columns]
            )
            if turn == 0:
                windows[:, columns] = product
            else:
                windows[:, columns] = windows[:, columns] + product

    def neighbours(tail_source, tail, head_source, head, sem):
        return (
            pltpu.make_async_remote_copy(
                src_ref=tail_source,
                dst_ref=tail,
                send_sem=sem.at[0],
                recv_sem=sem.at[1],
                device_id=to_seg(after),
                device_id_type=MESH,
            ),
            pltpu.make_async_remote_copy(
                src_ref=head_source,
                dst_ref=head,
                send_sem=sem.at[2],
                recv_sem=sem.at[3],
                device_id=to_seg(before),
                device_id_type=MESH,
            ),
        )

    def joined(own, tail, head):
        before_us = jnp.where(work == 0, 0.0, tail)
        hop = lax.broadcasted_iota(jnp.int32, head.shape, 1)
        after_us = jnp.where(hop < 3, head, 0.0)
        one, two = own[:2], own[2:]
        spill = one[:, HOPS:]
        middle = jnp.where(hop < 3, spill + two[:, :8], 0.0)
        one = jnp.concatenate([one[:, :8] + before_us, one[:, 8:HOPS], middle], axis=1)
        two = jnp.concatenate(
            [two[:, :8] + spill, two[:, 8:HOPS], two[:, HOPS:] + after_us], axis=1
        )
        whole = jnp.concatenate([one, two], axis=0)
        return jnp.where(inside, whole.reshape(ROWS, HOP), 0.0)

    est_own[...] = overlap_add(windows).reshape(LOCAL_CLIPS, 32, HOP)
    est_copies = neighbours(
        est_own.at[pl.ds(2, 2), pl.ds(HOPS, 8), :],
        est_tail,
        est_own.at[pl.ds(0, 2), pl.ds(0, 8), :],
        est_head,
        est_sem,
    )
    for copy in est_copies:
        copy.start()

    pltpu.make_async_copy(tgt_raw, tgt, tgt_sem.at[1]).wait()
    pltpu.make_async_copy(tgt_next, tgt_next, tgt_sem.at[5]).wait()
    own = tgt[...].astype(F32)
    first_half = jnp.concatenate([own[:2], own[2:, :8]], axis=1)
    second_half = jnp.concatenate([own[2:], tgt_next[...]], axis=1)
    own = jnp.concatenate([first_half, second_half], axis=0).reshape(ROWS, HOP)
    write_windows(tgt_win, jnp.where(inside, own, 0.0))

    def frames_of(windows_ref, points):
        stride = points // 4
        parts = [
            windows_ref[:, at * stride : at * stride + points] for at in range(HOP // stride)
        ]
        return parts[0] if len(parts) == 1 else jnp.concatenate(parts, axis=0)

    for level, points in enumerate(SIZES):
        half = points // 2
        count = NFFT // points
        table_copies[level].wait()

        def target_columns(step, energy, level=level, points=points, half=half, count=count):
            column = pl.multiple_of(step * 256, 256)
            frames = frames_of(tgt_win, points)
            real = matmul(frames, analysis[level][:, pl.ds(column, 256)])
            imag = matmul(frames, analysis[level][:, pl.ds(half + column, 256)])
            power = real * real + imag * imag + EPS_MAG
            for at in range(count):
                place = pl.ds(pl.multiple_of(at * half + column, 256), 256)
                part = power[at * ROWS : (at + 1) * ROWS]
                tgt_mag[level, :, place] = jnp.sqrt(part)
                tgt_log[level, :, place] = 0.5 * jnp.log(part)
                energy = energy + fold_rows(jnp.where(usable, part, 0.0))
            return energy

        start = jnp.zeros((LOCAL_CLIPS, 8, 128), F32)
        sums[3 + level] = lax.fori_loop(0, half // 256, target_columns, start)

    for copy in est_copies:
        copy.wait_recv()
    write_windows(est_win, joined(est_own[...], est_tail[...], est_head[...]))

    for level, points in enumerate(SIZES):
        half = points // 2
        count = NFFT // points
        spread = jnp.zeros((LOCAL_CLIPS, 8, 128), F32)
        logterm = jnp.zeros((LOCAL_CLIPS, 8, 128), F32)
        for column in range(0, half, 256):
            frames = frames_of(est_win, points)
            all_real = matmul(frames, analysis[level][:, column : column + 256])
            all_imag = matmul(frames, analysis[level][:, half + column : half + column + 256])
            for at in range(count):
                rows = slice(at * ROWS, (at + 1) * ROWS)
                real, imag = all_real[rows], all_imag[rows]
                power = real * real + imag * imag + EPS_MAG
                inverse = lax.rsqrt(power)
                place = slice(at * half + column, at * half + column + 256)
                gap = power * inverse - tgt_mag[level, :, place]
                log_gap = 0.5 * jnp.log(power) - tgt_log[level, :, place]
                mag_factor = jnp.where(usable, gap * inverse, 0.0)
                log_factor = jnp.where(usable, log_gap * inverse * inverse * log_weight, 0.0)
                for part, first in (
                    (real, at * points + column),
                    (imag, at * points + half + column),
                ):
                    lanes = slice(first, first + 256)
                    grad_x[level, :ROWS, lanes] = (mag_factor * part).astype(BF16)
                    grad_x[level, ROWS:, lanes] = (log_factor * part).astype(BF16)
                spread = spread + fold_rows(jnp.where(usable, gap * gap, 0.0))
                logterm = logterm + fold_rows(jnp.where(usable, log_gap * log_gap, 0.0))
        sums[level] = spread
        sums[6 + level] = logterm

    flat = sums[...].reshape(36, 8, 128).sum(axis=1)
    flat = jnp.sum(flat, axis=1, keepdims=True)
    lane = lax.broadcasted_iota(jnp.int32, (36, 128), 1)
    line = lax.broadcasted_iota(jnp.int32, (36, 128), 0)
    own_stats = jnp.sum(jnp.where(lane == line, flat, 0.0), axis=0, keepdims=True)
    stat_send[...] = own_stats
    stat_recv[work] = own_stats

    def send_stats(step, carry):
        pltpu.make_async_remote_copy(
            src_ref=stat_send,
            dst_ref=stat_recv.at[work],
            send_sem=stat_sem.at[0],
            recv_sem=stat_sem.at[1],
            device_id=to_seg(device_of(lax.rem(work + step, WORKS), side)),
            device_id_type=MESH,
        ).start()
        return carry

    lax.fori_loop(1, WORKS, send_stats, 0)
    def add_to(ref, first, product):
        ref[:, first : first + 256] = ref[:, first : first + 256] + product

    for step in range(0, NFFT, 256):
        product = matmul_nt(grad_x[2], a2048[step : step + 256, :])
        mag_windows[2, :, step : step + 256] = product[:ROWS]
        windows[:, step : step + 256] = product[ROWS:]
    for level, points in ((1, 1024), (0, 512)):
        count = NFFT // points
        stacked = jnp.concatenate(
            [grad_x[level, :, at * points : (at + 1) * points] for at in range(count)], axis=0
        )
        for step in range(0, points, 256):
            product = matmul_nt(stacked, analysis[level][step : step + 256, :])
            for at in range(count):
                first = at * (points // 4) + step
                base = at * 2 * ROWS
                add_to(mag_windows.at[level], first, product[base : base + ROWS])
                add_to(windows, first, product[base + ROWS : base + 2 * ROWS])

    for level in range(3):
        grad_own[level] = overlap_add(mag_windows.at[level], level + 2)
    grad_own[3] = overlap_add(windows)
    hop8 = lax.broadcasted_iota(jnp.int32, (2, 8, HOP), 1)
    for pair in range(2):
        upper = grad_own[2 * pair].reshape(LOCAL_CLIPS, 32, HOP)
        lower = grad_own[2 * pair + 1].reshape(LOCAL_CLIPS, 32, HOP)
        tail_send[pair] = jnp.where(
            hop8 < 4, upper[2:, HOPS:], pltpu.roll(lower[2:, HOPS:], 4, 1)
        )
        head_send[pair] = jnp.where(hop8 < 4, upper[:2, :8], pltpu.roll(lower[:2, :8], 4, 1))
    grad_copies = neighbours(tail_send, grad_tail, head_send, grad_head, grad_sem)
    for copy in grad_copies:
        copy.start()

    others = stat_recv.at[pl.ds(0, WORKS - 1)]
    pltpu.make_async_copy(others, others, stat_sem.at[1]).wait()
    totals = stat_recv[...].sum(axis=0)

    place = lax.broadcasted_iota(jnp.int32, (1, 128), 1)
    low_half = lax.rem(place, 4) < 2
    totals = totals + jnp.where(low_half, pltpu.roll(totals, 126, 1), pltpu.roll(totals, 2, 1))
    energy = pltpu.roll(totals, 128 - 12, 1)
    logterm = pltpu.roll(totals, 128 - 24, 1)
    filled = place < 12
    lane_length = jnp.where(
        lax.rem(place, 2) == 0, lengths_ref[2 * side], lengths_ref[2 * side + 1]
    )
    entries = (lane_length * BINS).astype(F32)
    safe_energy = jnp.where(filled, energy, 1.0)
    safe_spread = jnp.where(filled, totals, 1.0) + EPS_RATIO
    terms = jnp.where(filled & low_half, jnp.sqrt(safe_spread / safe_energy) + logterm / entries, 0.0)
    weights = SCALE / jnp.sqrt(safe_spread * safe_energy)
    weights = jnp.broadcast_to(weights, (ROWS, 128))
    pick_lane = lax.broadcasted_iota(jnp.int32, (ROWS, 128), 1)
    pick_row = lax.broadcasted_iota(jnp.int32, (ROWS, 128), 0) // 32
    mag_weights = [
        jnp.sum(jnp.where(pick_lane == level * 4 + pick_row, weights, 0.0), axis=1, keepdims=True)
        for level in range(3)
    ]
    own = grad_own[3]
    for level in range(3):
        own = own + mag_weights[level] * grad_own[level]
    for copy in grad_copies:
        copy.wait_recv()

    def weighted(received):
        def row_of(component):
            block = received[component // 2]
            return block if component % 2 == 0 else pltpu.roll(block, 4, 1)

        total = row_of(3)
        for level in range(3):
            weight = mag_weights[level].reshape(LOCAL_CLIPS, 32, 1)[:2, :8]
            total = total + weight * row_of(level)
        return jnp.where(hop8 < 3, total, 0.0)

    write_windows(
        grad_win,
        joined(own.reshape(LOCAL_CLIPS, 32, HOP), weighted(grad_tail), weighted(grad_head)),
    )

    first_tile = me // 8 + 1

    def back_bins(step, carry):
        tile = lax.rem(first_tile + step, 8)
        product = matmul_nt(grad_win[...], syn[pl.ds(pl.multiple_of(tile * 256, 256), 256), :])
        for g in range(2):
            lanes = product[:, g * 128 : (g + 1) * 128]
            by_clip = [lanes[c * 32 : c * 32 + HOPS] for c in range(LOCAL_CLIPS)]
            for i, block in enumerate(swap_lane_groups(by_clip)):
                send_out[tile * 8 + g * 4 + i] = block.astype(BF16)
        for i in range(8):
            there = tile * 8 + i

            @pl.when(there != me)
            def _():
                pltpu.make_async_remote_copy(
                    src_ref=send_out.at[there],
                    dst_ref=recv_out.at[my_slot],
                    send_sem=out_send_sem,
                    recv_sem=out_recv_sem.at[my_chunk],
                    device_id=to_seg(there),
                    device_id_type=MESH,
                ).start()

            @pl.when(there == me)
            def _():
                pltpu.make_async_copy(
                    send_out.at[me], recv_out.at[my_slot], out_recv_sem.at[my_chunk]
                ).start()

        return carry

    lax.fori_loop(0, 8, back_bins, 0)

    own_loss = jnp.sum(terms, axis=1, keepdims=True) + jnp.zeros((1, 128), F32)
    loss_send[...] = own_loss
    my_loss = clip * 2 + side
    loss_recv[my_loss] = own_loss
    for peer in loss_peers:
        pltpu.make_async_remote_copy(
            src_ref=loss_send,
            dst_ref=loss_recv.at[my_loss],
            send_sem=loss_sem.at[0],
            recv_sem=loss_sem.at[1],
            device_id=peer,
            device_id_type=MESH,
        ).start()

    seven = loss_recv.at[pl.ds(0, 2 * CLIP_GROUPS - 1)]
    pltpu.make_async_copy(seven, seven, loss_sem.at[1]).wait()
    loss_ref[...] = loss_recv[...].sum(axis=0) / (3 * CLIPS)

    for turn in range(4):
        chunk = lax.rem(my_chunk + (3 - turn), 4)
        slabs = pl.ds(pl.multiple_of(chunk * SLABS, SLABS), SLABS)
        pltpu.make_async_copy(
            send_out.at[slabs], recv_out.at[slabs], out_recv_sem.at[chunk]
        ).wait()
        arrived = recv_out[slabs].astype(F32)
        one, two = halves(arrived[:8], arrived[8:])
        whole = jnp.concatenate([one[:, None], two[:, None]], axis=1)
        turned = whole.reshape(SLABS * HOPS, 128).T
        out_ref[:, pl.ds(pl.multiple_of(chunk * 384, 128), 384)] = turned.astype(BF16)

    for copy in est_copies + grad_copies + (tgt_across,):
        copy.wait_send()

    @pl.when(jnp.logical_not(near_stays))
    def _():
        pltpu.make_async_copy(near_source, near_source, tgt_sem.at[2]).wait()

    for at, (source, there) in enumerate(heads):

        @pl.when((core == 0) & (there != me))
        def _(at=at):
            pltpu.make_async_copy(tgt_next, tgt_next, tgt_sem.at[3 + at]).wait()

    pltpu.make_async_copy(others, others, stat_sem.at[0]).wait()
    pltpu.make_async_copy(seven, seven, loss_sem.at[0]).wait()
    sent = pl.ds(0, SEGS - 1)
    pltpu.make_async_copy(send_in.at[sent], recv_in.at[sent], in_send_sem).wait()
    pltpu.make_async_copy(send_out.at[sent], recv_out.at[sent], out_send_sem).wait()


def body(spectra, target, lengths):
    vmem = pl.BlockSpec(memory_space=pltpu.VMEM)
    smem = pl.BlockSpec(memory_space=pltpu.SMEM)
    anywhere = pl.BlockSpec(memory_space=pl.ANY)
    slabs = pltpu.VMEM((SEGS, HOPS, 128), BF16)
    pairs = pltpu.VMEM((2, 2, 8, HOP), F32)
    hops8 = pltpu.VMEM((2, 8, HOP), F32)
    hops24 = pltpu.VMEM((LOCAL_CLIPS, HOPS, HOP), BF16)
    hops32 = pltpu.VMEM((LOCAL_CLIPS, 32, HOP), F32)
    window = pltpu.VMEM((ROWS, NFFT), BF16)
    entries = pltpu.VMEM((3, ROWS, BINS), F32)
    dma = pltpu.SemaphoreType.DMA
    out, loss = pl.pallas_call(
        kernel,
        out_shape=(
            jax.ShapeDtypeStruct((ROWS, FRAMES), BF16),
            jax.ShapeDtypeStruct((1, 128), F32),
        ),
        in_specs=[vmem, vmem, smem] + [anywhere] * 4,
        out_specs=(vmem, vmem),
        scratch_shapes=[
            slabs, slabs, pltpu.VMEM((ROWS, 512), BF16), slabs, slabs,
            pltpu.VMEM((LOCAL_CLIPS, HOPS, HOP), F32), hops24, hops8,
            pltpu.VMEM((2048, 2048), BF16), pltpu.VMEM((512, 512), BF16),
            pltpu.VMEM((1024, 1024), BF16), pltpu.VMEM((2048, 2048), BF16),
            hops24, window, hops32, hops8, hops8, window,
            pltpu.VMEM((ROWS, NFFT), F32), pltpu.VMEM((3, ROWS, NFFT), F32), entries, entries,
            pltpu.VMEM((3, 2 * ROWS, NFFT), BF16),
            pltpu.VMEM((4, ROWS, HOP), F32), pairs, pairs, pairs, pairs, window,
            pltpu.VMEM((9, LOCAL_CLIPS, 8, 128), F32),
            pltpu.VMEM((1, 128), F32), pltpu.VMEM((WORKS, 1, 128), F32),
            pltpu.VMEM((1, 128), F32), pltpu.VMEM((2 * CLIP_GROUPS, 1, 128), F32),
            dma((4,)), dma, dma((4,)), dma, dma((4,)),
            dma((6,)), dma((4,)), dma((4,)), dma((2,)), dma((2,)),
        ],
        compiler_params=pltpu.CompilerParams(
            collective_id=0, has_side_effects=True, vmem_limit_bytes=60 * 2**20
        ),
        cost_estimate=pl.CostEstimate(
            flops=8 * 10**9, bytes_accessed=20 * 10**6, transcendentals=10**6
        ),
    )(
        spectra.reshape(ROWS, FRAMES),
        target,
        lengths,
        jnp.asarray(synthesis_table()),
        *(jnp.asarray(analysis_table(points)) for points in SIZES),
    )
    return loss[0, 0], out.reshape(LOCAL_CLIPS, 2, BINS // SEGS, FRAMES)


def solution(mesh):
    placed = (P("clip", None, "seg", None), P("clip", "seg"), P("clip"))
    return jax.shard_map(
        body,
        mesh=mesh,
        in_specs=placed,
        out_specs=(P(), P("clip", None, "seg", None)),
        check_vma=False,
    )
```

```python
import math

import jax
import jax.numpy as jnp
import ml_dtypes
import numpy as np
from jax import lax
from jax.experimental import pallas as pl
from jax.experimental.pallas import tpu as pltpu
from jax.sharding import PartitionSpec as P

BINS = 1024
NFFT = 2048
HOP = 512
FRAMES = 1536
CLIPS = 16
SEGS = 64
WORKS = 32
CLIP_GROUPS = 4
LOCAL_CLIPS = 4
HOPS = 24
ROWS = 128
SLABS = 16
EPS_MAG = 0.1
EPS_RATIO = 1e-05
SIZES = (512, 1024, 2048)
SCALE = float(FRAMES * BINS)
F32 = jnp.float32
BF16 = jnp.bfloat16
MESH = pl.DeviceIdType.MESH


def wave_table(bins_index, time_index, points, factor):
    halfway = points // 2
    is_sine = bins_index >= halfway
    harmonic = np.where(is_sine, bins_index - halfway, bins_index)
    angles = (harmonic * time_index % points).astype(np.float32) * np.float32(2.0 * math.pi / points)
    window = np.float32(0.5) - np.float32(0.5) * np.cos(
        time_index.astype(np.float32) * np.float32(2.0 * math.pi / points)
    )
    entry_value = np.where(is_sine, -np.sin(angles), np.cos(angles))
    return (entry_value * window * np.float32(factor)).astype(ml_dtypes.bfloat16)


def analysis_table(points):
    index = np.arange(points, dtype=np.int32)
    return wave_table(index[None, :], index[:, None], points, 1.0 / math.sqrt(points))


def synthesis_table():
    owner, part, bin_at = np.meshgrid(np.arange(64), np.arange(2), np.arange(16), indexing="ij")
    index = (part * BINS + owner * 16 + bin_at).reshape(-1).astype(np.int32)
    time = np.arange(NFFT, dtype=np.int32)
    return wave_table(index[:, None], time[None, :], NFFT, 1.0 / math.sqrt(BINS))


def to_seg(index):
    return {"seg": index}


def matmul(a, b):
    return lax.dot_general(a, b, (((1,), (0,)), ((), ())), preferred_element_type=F32)


def matmul_nt(a, b):
    return lax.dot_general(a, b, (((1,), (1,)), ((), ())), preferred_element_type=F32)


def swap_lane_groups(tiles):
    lane = lax.broadcasted_iota(jnp.int32, tiles[0].shape, 1) // 32
    results = []
    for j in range(4):
        result = tiles[j]
        for i in range(4):
            if i != j:
                moved = pltpu.roll(tiles[i], (32 * (i - j)) % 128, 1)
                result = jnp.where(lane == i, moved, result)
        results.append(result)
    return results


def overlap_add(windows_ref, quarters=4):
    total = windows_ref[:, :HOP]
    for q in range(1, quarters):
        total = total + pltpu.roll(windows_ref[:, q * HOP : (q + 1) * HOP], q, 0)
    return total


def write_windows(windows_ref, wave):
    windows_ref[:, :HOP] = wave.astype(BF16)
    for q in range(1, 4):
        windows_ref[:, q * HOP : (q + 1) * HOP] = pltpu.roll(wave, ROWS - q, 0).astype(BF16)


def halves(first, second):
    shape = first.shape
    first, second = first.reshape(-1, 128), second.reshape(-1, 128)
    low = lax.broadcasted_iota(jnp.int32, first.shape, 1) < 64
    one = jnp.where(low, first, pltpu.roll(second, 64, 1))
    other = jnp.where(low, pltpu.roll(first, 64, 1), second)
    return one.reshape(shape), other.reshape(shape)


def fold_rows(tile):
    by_clip = tile.reshape(LOCAL_CLIPS, 4, 8, tile.shape[1]).sum(axis=1)
    return by_clip[:, :, :128] + by_clip[:, :, 128:]


def kernel(
    spec_ref, target_ref, lengths_ref, syn_hbm, a512_hbm, a1024_hbm, a2048_hbm,
    out_ref, loss_ref,
    send_in, recv_in, chunk_in, send_out, recv_out, tgt_rows, tgt_raw, tgt_next,
    syn, a512, a1024, a2048,
    tgt, tgt_win, est_own, est_tail, est_head, est_win,
    windows, mag_windows, tgt_mag, tgt_log, grad_x,
    grad_own, tail_send, head_send, grad_tail, grad_head, grad_win,
    sums, stat_send, stat_recv, loss_send, loss_recv,
    table_sem, in_send_sem, in_recv_sem, out_send_sem, out_recv_sem,
    tgt_sem, est_sem, grad_sem, stat_sem, loss_sem,
):
    me = lax.axis_index("seg")
    clip = lax.axis_index("clip")
    analysis = (a512, a1024, a2048)
    spot = me // 4
    core = lax.rem(me, 2)
    side = lax.rem(me // 2, 2)
    work = spot * 2 + core

    def device_of(work_index, side_index):
        return (work_index // 2) * 4 + side_index * 2 + lax.rem(work_index, 2)

    def slot_of(work_index, side_index):
        return (work_index // 8) * 16 + side_index * 8 + lax.rem(work_index, 8)

    after = device_of(lax.rem(work + 1, WORKS), side)
    before = device_of(lax.rem(work + WORKS - 1, WORKS), side)
    my_slot = slot_of(work, side)
    loss_peers = [
        (lax.rem(clip + step // 2, CLIP_GROUPS), device_of(work, lax.rem(side + step, 2)))
        for step in range(1, 2 * CLIP_GROUPS)
    ]

    barrier = pltpu.get_barrier_semaphore()

    def greet(step, carry):
        pl.semaphore_signal(
            barrier, inc=1, device_id=to_seg(lax.rem(me + step, SEGS)), device_id_type=MESH
        )
        return carry

    lax.fori_loop(1, SEGS, greet, 0)
    for peer in loss_peers[1:]:
        pl.semaphore_signal(barrier, inc=1, device_id=peer, device_id_type=MESH)

    table_copies = [
        pltpu.make_async_copy(source, held, table_sem.at[at])
        for at, (source, held) in enumerate(
            ((a512_hbm, a512), (a1024_hbm, a1024), (a2048_hbm, a2048), (syn_hbm, syn))
        )
    ]
    for copy in table_copies:
        copy.start()

    for hop in range(HOPS):
        tgt_rows[:, hop, :] = target_ref[:, hop * HOP : (hop + 1) * HOP].astype(F32)
    tgt_raw[...] = tgt_rows[...].astype(BF16)
    for part in range(4):
        turned = spec_ref[:, 384 * part : 384 * (part + 1)].astype(F32).T
        turned = turned.reshape(8, 2, HOPS, 128)
        for at, message in enumerate(halves(turned[:, 0], turned[:, 1])):
            first = part * 16 + at * 8
            send_in[first : first + 8] = message.astype(BF16)

    pl.semaphore_wait(barrier, SEGS - 1 + len(loss_peers) - 1)

    my_chunk = me // SLABS

    def send_bins(step, to_side):
        there_work = lax.rem(work + step, WORKS)
        pltpu.make_async_remote_copy(
            src_ref=send_in.at[slot_of(there_work, to_side)],
            dst_ref=recv_in.at[me],
            send_sem=in_send_sem,
            recv_sem=in_recv_sem.at[my_chunk],
            device_id=to_seg(device_of(there_work, to_side)),
            device_id_type=MESH,
        ).start()
        return to_side

    lax.fori_loop(0, WORKS, send_bins, 1 - side)


    def hold(to_side):
        return tgt_raw.at[pl.ds(2 * to_side, 2)], tgt.at[pl.ds(2 * core, 2)]

    across_source, across_place = hold(1 - side)
    tgt_across = pltpu.make_async_remote_copy(
        src_ref=across_source,
        dst_ref=across_place,
        send_sem=tgt_sem.at[0],
        recv_sem=tgt_sem.at[1],
        device_id=to_seg(spot * 4 + (1 - side) * 2 + side),
        device_id_type=MESH,
    )
    tgt_across.start()
    lax.fori_loop(1, WORKS, send_bins, side)
    pltpu.make_async_copy(send_in.at[my_slot], recv_in.at[me], in_recv_sem.at[my_chunk]).start()
    near_source, near_place = hold(side)
    near_stays = core == side

    @pl.when(near_stays)
    def _():
        pltpu.make_async_copy(near_source, near_place, tgt_sem.at[1]).start()

    @pl.when(jnp.logical_not(near_stays))
    def _():
        pltpu.make_async_remote_copy(
            src_ref=near_source,
            dst_ref=near_place,
            send_sem=tgt_sem.at[2],
            recv_sem=tgt_sem.at[1],
            device_id=to_seg(spot * 4 + side * 3),
            device_id_type=MESH,
        ).start()

    ahead = lax.rem(spot * 2 + side + WORKS - 1, WORKS)
    heads = [
        (tgt_rows.at[pl.ds(2 * to_side, 2), pl.ds(0, 8), :], device_of(ahead, to_side))
        for to_side in range(2)
    ]
    for at, (source, there) in enumerate(heads):

        @pl.when((core == 0) & (there != me))
        def _(at=at, source=source, there=there):
            pltpu.make_async_remote_copy(
                src_ref=source,
                dst_ref=tgt_next,
                send_sem=tgt_sem.at[3 + at],
                recv_sem=tgt_sem.at[5],
                device_id=to_seg(there),
                device_id_type=MESH,
            ).start()

        @pl.when((core == 0) & (there == me))
        def _(source=source):
            pltpu.make_async_copy(source, tgt_next, tgt_sem.at[5]).start()

    row = lax.broadcasted_iota(jnp.int32, (ROWS, 1), 0)
    row_clip = row // 32
    row_hop = lax.rem(row, 32)
    row_length = jnp.where(
        lax.rem(row_clip, 2) == 0, lengths_ref[2 * side], lengths_ref[2 * side + 1]
    )
    inside = work * (2 * HOPS) + (row_clip // 2) * HOPS + row_hop < row_length
    usable = inside & (row_hop < HOPS)
    log_weight = (2.0 * SCALE) / (row_length * BINS).astype(F32)
    for level in range(2):
        mag_windows[level] = jnp.zeros((ROWS, NFFT), F32)

    table_copies[3].wait()
    for turn in range(4):
        chunk = lax.rem(my_chunk + (3 - turn), 4)
        slabs = pl.ds(pl.multiple_of(chunk * SLABS, SLABS), SLABS)
        pltpu.make_async_copy(
            send_in.at[slabs], recv_in.at[slabs], in_recv_sem.at[chunk]
        ).wait()
        arrived = recv_in[slabs].astype(F32).reshape(4, 4, HOPS, 128)
        by_source = [arrived[:, i].reshape(4 * HOPS, 128) for i in range(4)]
        by_clip = swap_lane_groups(by_source)
        for c in range(LOCAL_CLIPS):
            for g in range(4):
                block = by_clip[c][g * HOPS : (g + 1) * HOPS]
                block = jnp.concatenate([block, jnp.zeros((8, 128), F32)], axis=0)
                chunk_in[c * 32 : (c + 1) * 32, g * 128 : (g + 1) * 128] = block.astype(BF16)
        for tile in range(4):
            columns = slice(tile * 512, (tile + 1) * 512)
            product = matmul(
                chunk_in[...], syn[pl.ds(pl.multiple_of(chunk * 512, 512), 512), columns]
            )
            if turn == 0:
                windows[:, columns] = product
            else:
                windows[:, columns] = windows[:, columns] + product

    def neighbours(tail_source, tail, head_source, head, sem):
        return (
            pltpu.make_async_remote_copy(
                src_ref=tail_source,
                dst_ref=tail,
                send_sem=sem.at[0],
                recv_sem=sem.at[1],
                device_id=to_seg(after),
                device_id_type=MESH,
            ),
            pltpu.make_async_remote_copy(
                src_ref=head_source,
                dst_ref=head,
                send_sem=sem.at[2],
                recv_sem=sem.at[3],
                device_id=to_seg(before),
                device_id_type=MESH,
            ),
        )

    def joined(own, tail, head):
        before_us = jnp.where(work == 0, 0.0, tail)
        hop = lax.broadcasted_iota(jnp.int32, head.shape, 1)
        after_us = jnp.where(hop < 3, head, 0.0)
        one, two = own[:2], own[2:]
        spill = one[:, HOPS:]
        middle = jnp.where(hop < 3, spill + two[:, :8], 0.0)
        one = jnp.concatenate([one[:, :8] + before_us, one[:, 8:HOPS], middle], axis=1)
        two = jnp.concatenate(
            [two[:, :8] + spill, two[:, 8:HOPS], two[:, HOPS:] + after_us], axis=1
        )
        whole = jnp.concatenate([one, two], axis=0)
        return jnp.where(inside, whole.reshape(ROWS, HOP), 0.0)

    est_own[...] = overlap_add(windows).reshape(LOCAL_CLIPS, 32, HOP)
    est_copies = neighbours(
        est_own.at[pl.ds(2, 2), pl.ds(HOPS, 8), :],
        est_tail,
        est_own.at[pl.ds(0, 2), pl.ds(0, 8), :],
        est_head,
        est_sem,
    )
    for copy in est_copies:
        copy.start()

    pltpu.make_async_copy(tgt_raw, tgt, tgt_sem.at[1]).wait()
    pltpu.make_async_copy(tgt_next, tgt_next, tgt_sem.at[5]).wait()
    own = tgt[...].astype(F32)
    first_half = jnp.concatenate([own[:2], own[2:, :8]], axis=1)
    second_half = jnp.concatenate([own[2:], tgt_next[...]], axis=1)
    own = jnp.concatenate([first_half, second_half], axis=0).reshape(ROWS, HOP)
    write_windows(tgt_win, jnp.where(inside, own, 0.0))

    def frames_of(windows_ref, points):
        stride = points // 4
        parts = [
            windows_ref[:, at * stride : at * stride + points] for at in range(HOP // stride)
        ]
        return parts[0] if len(parts) == 1 else jnp.concatenate(parts, axis=0)

    for level, points in enumerate(SIZES):
        half = points // 2
        count = NFFT // points
        table_copies[level].wait()

        def target_columns(step, energy, level=level, points=points, half=half, count=count):
            column = pl.multiple_of(step * 256, 256)
            frames = frames_of(tgt_win, points)
            real = matmul(frames, analysis[level][:, pl.ds(column, 256)])
            imag = matmul(frames, analysis[level][:, pl.ds(half + column, 256)])
            power = real * real + imag * imag + EPS_MAG
            for at in range(count):
                place = pl.ds(pl.multiple_of(at * half + column, 256), 256)
                part = power[at * ROWS : (at + 1) * ROWS]
                tgt_mag[level, :, place] = jnp.sqrt(part)
                tgt_log[level, :, place] = 0.5 * jnp.log(part)
                energy = energy + fold_rows(jnp.where(usable, part, 0.0))
            return energy

        start = jnp.zeros((LOCAL_CLIPS, 8, 128), F32)
        sums[3 + level] = lax.fori_loop(0, half // 256, target_columns, start)

    for copy in est_copies:
        copy.wait_recv()
    write_windows(est_win, joined(est_own[...], est_tail[...], est_head[...]))

    for level, points in enumerate(SIZES):
        half = points // 2
        count = NFFT // points
        spread = jnp.zeros((LOCAL_CLIPS, 8, 128), F32)
        logterm = jnp.zeros((LOCAL_CLIPS, 8, 128), F32)
        for column in range(0, half, 256):
            frames = frames_of(est_win, points)
            all_real = matmul(frames, analysis[level][:, column : column + 256])
            all_imag = matmul(frames, analysis[level][:, half + column : half + column + 256])
            for at in range(count):
                rows = slice(at * ROWS, (at + 1) * ROWS)
                real, imag = all_real[rows], all_imag[rows]
                power = real * real + imag * imag + EPS_MAG
                inverse = lax.rsqrt(power)
                place = slice(at * half + column, at * half + column + 256)
                gap = power * inverse - tgt_mag[level, :, place]
                log_gap = 0.5 * jnp.log(power) - tgt_log[level, :, place]
                mag_factor = jnp.where(usable, gap * inverse, 0.0)
                log_factor = jnp.where(usable, log_gap * inverse * inverse * log_weight, 0.0)
                for part, first in (
                    (real, at * points + column),
                    (imag, at * points + half + column),
                ):
                    lanes = slice(first, first + 256)
                    grad_x[level, :ROWS, lanes] = (mag_factor * part).astype(BF16)
                    grad_x[level, ROWS:, lanes] = (log_factor * part).astype(BF16)
                spread = spread + fold_rows(jnp.where(usable, gap * gap, 0.0))
                logterm = logterm + fold_rows(jnp.where(usable, log_gap * log_gap, 0.0))
        sums[level] = spread
        sums[6 + level] = logterm

    flat = sums[...].reshape(36, 8, 128).sum(axis=1)
    flat = jnp.sum(flat, axis=1, keepdims=True)
    lane = lax.broadcasted_iota(jnp.int32, (36, 128), 1)
    line = lax.broadcasted_iota(jnp.int32, (36, 128), 0)
    own_stats = jnp.sum(jnp.where(lane == line, flat, 0.0), axis=0, keepdims=True)
    stat_send[...] = own_stats
    stat_recv[work] = own_stats

    def send_stats(step, carry):
        pltpu.make_async_remote_copy(
            src_ref=stat_send,
            dst_ref=stat_recv.at[work],
            send_sem=stat_sem.at[0],
            recv_sem=stat_sem.at[1],
            device_id=to_seg(device_of(lax.rem(work + step, WORKS), side)),
            device_id_type=MESH,
        ).start()
        return carry

    lax.fori_loop(1, WORKS, send_stats, 0)
    def add_to(ref, first, product):
        ref[:, first : first + 256] = ref[:, first : first + 256] + product

    for step in range(0, NFFT, 256):
        product = matmul_nt(grad_x[2], a2048[step : step + 256, :])
        mag_windows[2, :, step : step + 256] = product[:ROWS]
        windows[:, step : step + 256] = product[ROWS:]
    for level, points in ((1, 1024), (0, 512)):
        count = NFFT // points
        stacked = jnp.concatenate(
            [grad_x[level, :, at * points : (at + 1) * points] for at in range(count)], axis=0
        )
        for step in range(0, points, 256):
            product = matmul_nt(stacked, analysis[level][step : step + 256, :])
            for at in range(count):
                first = at * (points // 4) + step
                base = at * 2 * ROWS
                add_to(mag_windows.at[level], first, product[base : base + ROWS])
                add_to(windows, first, product[base + ROWS : base + 2 * ROWS])

    for level in range(3):
        grad_own[level] = overlap_add(mag_windows.at[level], level + 2)
    grad_own[3] = overlap_add(windows)
    hop8 = lax.broadcasted_iota(jnp.int32, (2, 8, HOP), 1)
    for pair in range(2):
        upper = grad_own[2 * pair].reshape(LOCAL_CLIPS, 32, HOP)
        lower = grad_own[2 * pair + 1].reshape(LOCAL_CLIPS, 32, HOP)
        tail_send[pair] = jnp.where(
            hop8 < 4, upper[2:, HOPS:], pltpu.roll(lower[2:, HOPS:], 4, 1)
        )
        head_send[pair] = jnp.where(hop8 < 4, upper[:2, :8], pltpu.roll(lower[:2, :8], 4, 1))
    grad_copies = neighbours(tail_send, grad_tail, head_send, grad_head, grad_sem)
    for copy in grad_copies:
        copy.start()

    others = stat_recv.at[pl.ds(0, WORKS - 1)]
    pltpu.make_async_copy(others, others, stat_sem.at[1]).wait()
    totals = stat_recv[...].sum(axis=0)

    place = lax.broadcasted_iota(jnp.int32, (1, 128), 1)
    low_half = lax.rem(place, 4) < 2
    totals = totals + jnp.where(low_half, pltpu.roll(totals, 126, 1), pltpu.roll(totals, 2, 1))
    energy = pltpu.roll(totals, 128 - 12, 1)
    logterm = pltpu.roll(totals, 128 - 24, 1)
    filled = place < 12
    lane_length = jnp.where(
        lax.rem(place, 2) == 0, lengths_ref[2 * side], lengths_ref[2 * side + 1]
    )
    entries = (lane_length * BINS).astype(F32)
    safe_energy = jnp.where(filled, energy, 1.0)
    safe_spread = jnp.where(filled, totals, 1.0) + EPS_RATIO
    terms = jnp.where(filled & low_half, jnp.sqrt(safe_spread / safe_energy) + logterm / entries, 0.0)
    weights = SCALE / jnp.sqrt(safe_spread * safe_energy)
    weights = jnp.broadcast_to(weights, (ROWS, 128))
    pick_lane = lax.broadcasted_iota(jnp.int32, (ROWS, 128), 1)
    pick_row = lax.broadcasted_iota(jnp.int32, (ROWS, 128), 0) // 32
    mag_weights = [
        jnp.sum(jnp.where(pick_lane == level * 4 + pick_row, weights, 0.0), axis=1, keepdims=True)
        for level in range(3)
    ]
    own = grad_own[3]
    for level in range(3):
        own = own + mag_weights[level] * grad_own[level]
    for copy in grad_copies:
        copy.wait_recv()

    def weighted(received):
        def row_of(component):
            block = received[component // 2]
            return block if component % 2 == 0 else pltpu.roll(block, 4, 1)

        total = row_of(3)
        for level in range(3):
            weight = mag_weights[level].reshape(LOCAL_CLIPS, 32, 1)[:2, :8]
            total = total + weight * row_of(level)
        return jnp.where(hop8 < 3, total, 0.0)

    write_windows(
        grad_win,
        joined(own.reshape(LOCAL_CLIPS, 32, HOP), weighted(grad_tail), weighted(grad_head)),
    )

    first_tile = me // 8 + 1

    def back_bins(step, carry):
        tile = lax.rem(first_tile + step, 8)
        product = matmul_nt(grad_win[...], syn[pl.ds(pl.multiple_of(tile * 256, 256), 256), :])
        for g in range(2):
            lanes = product[:, g * 128 : (g + 1) * 128]
            by_clip = [lanes[c * 32 : c * 32 + HOPS] for c in range(LOCAL_CLIPS)]
            for i, block in enumerate(swap_lane_groups(by_clip)):
                send_out[tile * 8 + g * 4 + i] = block.astype(BF16)
        for i in range(8):
            to_side = 1 - side if i < 4 else side
            there = tile * 8 + (i // 2 % 2) * 4 + to_side * 2 + i % 2

            @pl.when(there != me)
            def _():
                pltpu.make_async_remote_copy(
                    src_ref=send_out.at[there],
                    dst_ref=recv_out.at[my_slot],
                    send_sem=out_send_sem,
                    recv_sem=out_recv_sem.at[my_chunk],
                    device_id=to_seg(there),
                    device_id_type=MESH,
                ).start()

            @pl.when(there == me)
            def _():
                pltpu.make_async_copy(
                    send_out.at[me], recv_out.at[my_slot], out_recv_sem.at[my_chunk]
                ).start()

        return carry

    lax.fori_loop(0, 8, back_bins, 0)

    own_loss = jnp.sum(terms, axis=1, keepdims=True) + jnp.zeros((1, 128), F32)
    loss_send[...] = own_loss
    my_loss = clip * 2 + side
    loss_recv[my_loss] = own_loss
    for peer in loss_peers:
        pltpu.make_async_remote_copy(
            src_ref=loss_send,
            dst_ref=loss_recv.at[my_loss],
            send_sem=loss_sem.at[0],
            recv_sem=loss_sem.at[1],
            device_id=peer,
            device_id_type=MESH,
        ).start()

    seven = loss_recv.at[pl.ds(0, 2 * CLIP_GROUPS - 1)]
    pltpu.make_async_copy(seven, seven, loss_sem.at[1]).wait()
    loss_ref[...] = loss_recv[...].sum(axis=0) / (3 * CLIPS)

    for turn in range(4):
        chunk = lax.rem(my_chunk + (3 - turn), 4)
        slabs = pl.ds(pl.multiple_of(chunk * SLABS, SLABS), SLABS)
        pltpu.make_async_copy(
            send_out.at[slabs], recv_out.at[slabs], out_recv_sem.at[chunk]
        ).wait()
        arrived = recv_out[slabs].astype(F32)
        one, two = halves(arrived[:8], arrived[8:])
        whole = jnp.concatenate([one[:, None], two[:, None]], axis=1)
        turned = whole.reshape(SLABS * HOPS, 128).T
        out_ref[:, pl.ds(pl.multiple_of(chunk * 384, 128), 384)] = turned.astype(BF16)

    for copy in est_copies + grad_copies + (tgt_across,):
        copy.wait_send()

    @pl.when(jnp.logical_not(near_stays))
    def _():
        pltpu.make_async_copy(near_source, near_source, tgt_sem.at[2]).wait()

    for at, (source, there) in enumerate(heads):

        @pl.when((core == 0) & (there != me))
        def _(at=at):
            pltpu.make_async_copy(tgt_next, tgt_next, tgt_sem.at[3 + at]).wait()

    pltpu.make_async_copy(others, others, stat_sem.at[0]).wait()
    pltpu.make_async_copy(seven, seven, loss_sem.at[0]).wait()
    sent = pl.ds(0, SEGS - 1)
    pltpu.make_async_copy(send_in.at[sent], recv_in.at[sent], in_send_sem).wait()
    pltpu.make_async_copy(send_out.at[sent], recv_out.at[sent], out_send_sem).wait()


def body(spectra, target, lengths):
    vmem = pl.BlockSpec(memory_space=pltpu.VMEM)
    smem = pl.BlockSpec(memory_space=pltpu.SMEM)
    anywhere = pl.BlockSpec(memory_space=pl.ANY)
    slabs = pltpu.VMEM((SEGS, HOPS, 128), BF16)
    pairs = pltpu.VMEM((2, 2, 8, HOP), F32)
    hops8 = pltpu.VMEM((2, 8, HOP), F32)
    hops24 = pltpu.VMEM((LOCAL_CLIPS, HOPS, HOP), BF16)
    hops32 = pltpu.VMEM((LOCAL_CLIPS, 32, HOP), F32)
    window = pltpu.VMEM((ROWS, NFFT), BF16)
    entries = pltpu.VMEM((3, ROWS, BINS), F32)
    dma = pltpu.SemaphoreType.DMA
    out, loss = pl.pallas_call(
        kernel,
        out_shape=(
            jax.ShapeDtypeStruct((ROWS, FRAMES), BF16),
            jax.ShapeDtypeStruct((1, 128), F32),
        ),
        in_specs=[vmem, vmem, smem] + [anywhere] * 4,
        out_specs=(vmem, vmem),
        scratch_shapes=[
            slabs, slabs, pltpu.VMEM((ROWS, 512), BF16), slabs, slabs,
            pltpu.VMEM((LOCAL_CLIPS, HOPS, HOP), F32), hops24, hops8,
            pltpu.VMEM((2048, 2048), BF16), pltpu.VMEM((512, 512), BF16),
            pltpu.VMEM((1024, 1024), BF16), pltpu.VMEM((2048, 2048), BF16),
            hops24, window, hops32, hops8, hops8, window,
            pltpu.VMEM((ROWS, NFFT), F32), pltpu.VMEM((3, ROWS, NFFT), F32), entries, entries,
            pltpu.VMEM((3, 2 * ROWS, NFFT), BF16),
            pltpu.VMEM((4, ROWS, HOP), F32), pairs, pairs, pairs, pairs, window,
            pltpu.VMEM((9, LOCAL_CLIPS, 8, 128), F32),
            pltpu.VMEM((1, 128), F32), pltpu.VMEM((WORKS, 1, 128), F32),
            pltpu.VMEM((1, 128), F32), pltpu.VMEM((2 * CLIP_GROUPS, 1, 128), F32),
            dma((4,)), dma, dma((4,)), dma, dma((4,)),
            dma((6,)), dma((4,)), dma((4,)), dma((2,)), dma((2,)),
        ],
        compiler_params=pltpu.CompilerParams(
            collective_id=0, has_side_effects=True, vmem_limit_bytes=60 * 2**20
        ),
        cost_estimate=pl.CostEstimate(
            flops=8 * 10**9, bytes_accessed=20 * 10**6, transcendentals=10**6
        ),
    )(
        spectra.reshape(ROWS, FRAMES),
        target,
        lengths,
        jnp.asarray(synthesis_table()),
        *(jnp.asarray(analysis_table(points)) for points in SIZES),
    )
    return loss[0, 0], out.reshape(LOCAL_CLIPS, 2, BINS // SEGS, FRAMES)


def solution(mesh):
    placed = (P("clip", None, "seg", None), P("clip", "seg"), P("clip"))
    return jax.shard_map(
        body,
        mesh=mesh,
        in_specs=placed,
        out_specs=(P(), P("clip", None, "seg", None)),
        check_vma=False,
    )
```

```python
import math

import jax
import jax.numpy as jnp
import ml_dtypes
import numpy as np
from jax import lax
from jax.experimental import pallas as pl
from jax.experimental.pallas import tpu as pltpu
from jax.sharding import PartitionSpec as P

BINS = 1024
NFFT = 2048
HOP = 512
FRAMES = 1536
CLIPS = 16
SEGS = 64
WORKS = 32
CLIP_GROUPS = 4
LOCAL_CLIPS = 4
HOPS = 24
ROWS = 128
SLABS = 16
EPS_MAG = 0.1
EPS_RATIO = 1e-05
SIZES = (512, 1024, 2048)
SCALE = float(FRAMES * BINS)
F32 = jnp.float32
BF16 = jnp.bfloat16
MESH = pl.DeviceIdType.MESH


def wave_table(bins_index, time_index, points, factor):
    halfway = points // 2
    is_sine = bins_index >= halfway
    harmonic = np.where(is_sine, bins_index - halfway, bins_index)
    angles = (harmonic * time_index % points).astype(np.float32) * np.float32(2.0 * math.pi / points)
    window = np.float32(0.5) - np.float32(0.5) * np.cos(
        time_index.astype(np.float32) * np.float32(2.0 * math.pi / points)
    )
    entry_value = np.where(is_sine, -np.sin(angles), np.cos(angles))
    return (entry_value * window * np.float32(factor)).astype(ml_dtypes.bfloat16)


def analysis_table(points):
    index = np.arange(points, dtype=np.int32)
    return wave_table(index[None, :], index[:, None], points, 1.0 / math.sqrt(points))


def synthesis_table():
    owner, part, bin_at = np.meshgrid(np.arange(64), np.arange(2), np.arange(16), indexing="ij")
    index = (part * BINS + owner * 16 + bin_at).reshape(-1).astype(np.int32)
    time = np.arange(NFFT, dtype=np.int32)
    return wave_table(index[:, None], time[None, :], NFFT, 1.0 / math.sqrt(BINS))


def to_seg(index):
    return {"seg": index}


def matmul(a, b):
    return lax.dot_general(a, b, (((1,), (0,)), ((), ())), preferred_element_type=F32)


def matmul_nt(a, b):
    return lax.dot_general(a, b, (((1,), (1,)), ((), ())), preferred_element_type=F32)


def swap_lane_groups(tiles):
    lane = lax.broadcasted_iota(jnp.int32, tiles[0].shape, 1) // 32
    results = []
    for j in range(4):
        result = tiles[j]
        for i in range(4):
            if i != j:
                moved = pltpu.roll(tiles[i], (32 * (i - j)) % 128, 1)
                result = jnp.where(lane == i, moved, result)
        results.append(result)
    return results


def overlap_add(windows_ref, quarters=4):
    total = windows_ref[:, :HOP]
    for q in range(1, quarters):
        total = total + pltpu.roll(windows_ref[:, q * HOP : (q + 1) * HOP], q, 0)
    return total


def write_windows(windows_ref, wave):
    windows_ref[:, :HOP] = wave.astype(BF16)
    for q in range(1, 4):
        windows_ref[:, q * HOP : (q + 1) * HOP] = pltpu.roll(wave, ROWS - q, 0).astype(BF16)


def halves(first, second):
    shape = first.shape
    first, second = first.reshape(-1, 128), second.reshape(-1, 128)
    low = lax.broadcasted_iota(jnp.int32, first.shape, 1) < 64
    one = jnp.where(low, first, pltpu.roll(second, 64, 1))
    other = jnp.where(low, pltpu.roll(first, 64, 1), second)
    return one.reshape(shape), other.reshape(shape)


def fold_rows(tile):
    by_clip = tile.reshape(LOCAL_CLIPS, 4, 8, tile.shape[1]).sum(axis=1)
    return by_clip[:, :, :128] + by_clip[:, :, 128:]


def kernel(
    spec_ref, target_ref, lengths_ref, syn_hbm, a512_hbm, a1024_hbm, a2048_hbm,
    out_ref, loss_ref,
    send_in, recv_in, chunk_in, send_out, recv_out, tgt_rows, tgt_raw, tgt_next,
    syn, a512, a1024, a2048,
    tgt, tgt_win, est_own, est_tail, est_head, est_win,
    windows, mag_windows, tgt_mag, tgt_log, grad_x,
    grad_own, tail_send, head_send, grad_tail, grad_head, grad_win,
    sums, stat_send, stat_recv, loss_send, loss_recv,
    table_sem, in_send_sem, in_recv_sem, out_send_sem, out_recv_sem,
    tgt_sem, est_sem, grad_sem, stat_sem, loss_sem,
):
    me = lax.axis_index("seg")
    clip = lax.axis_index("clip")
    analysis = (a512, a1024, a2048)
    spot = me // 4
    core = lax.rem(me, 2)
    side = lax.rem(me // 2, 2)
    work = spot * 2 + core

    def device_of(work_index, side_index):
        return (work_index // 2) * 4 + side_index * 2 + lax.rem(work_index, 2)

    def slot_of(work_index, side_index):
        return (work_index // 8) * 16 + side_index * 8 + lax.rem(work_index, 8)

    after = device_of(lax.rem(work + 1, WORKS), side)
    before = device_of(lax.rem(work + WORKS - 1, WORKS), side)
    my_slot = slot_of(work, side)
    loss_peers = [
        (lax.rem(clip + step // 2, CLIP_GROUPS), device_of(work, lax.rem(side + step, 2)))
        for step in range(1, 2 * CLIP_GROUPS)
    ]

    barrier = pltpu.get_barrier_semaphore()

    def greet(step, carry):
        pl.semaphore_signal(
            barrier, inc=1, device_id=to_seg(lax.rem(me + step, SEGS)), device_id_type=MESH
        )
        return carry

    lax.fori_loop(1, SEGS, greet, 0)
    for peer in loss_peers[1:]:
        pl.semaphore_signal(barrier, inc=1, device_id=peer, device_id_type=MESH)

    table_copies = [
        pltpu.make_async_copy(source, held, table_sem.at[at])
        for at, (source, held) in enumerate(
            ((a512_hbm, a512), (a1024_hbm, a1024), (a2048_hbm, a2048), (syn_hbm, syn))
        )
    ]
    for copy in table_copies:
        copy.start()

    for hop in range(HOPS):
        tgt_rows[:, hop, :] = target_ref[:, hop * HOP : (hop + 1) * HOP].astype(F32)
    tgt_raw[...] = tgt_rows[...].astype(BF16)
    for part in range(4):
        turned = spec_ref[:, 384 * part : 384 * (part + 1)].astype(F32).T
        turned = turned.reshape(8, 2, HOPS, 128)
        for at, message in enumerate(halves(turned[:, 0], turned[:, 1])):
            first = part * 16 + at * 8
            send_in[first : first + 8] = message.astype(BF16)

    pl.semaphore_wait(barrier, SEGS - 1 + len(loss_peers) - 1)

    my_chunk = me // SLABS

    def send_bins(step, carry):
        there = lax.rem(me + step, SEGS)
        pltpu.make_async_remote_copy(
            src_ref=send_in.at[
                slot_of((there // 4) * 2 + lax.rem(there, 2), lax.rem(there // 2, 2))
            ],
            dst_ref=recv_in.at[me],
            send_sem=in_send_sem,
            recv_sem=in_recv_sem.at[my_chunk],
            device_id=to_seg(there),
            device_id_type=MESH,
        ).start()
        return carry

    lax.fori_loop(1, SEGS, send_bins, 0)
    pltpu.make_async_copy(send_in.at[my_slot], recv_in.at[me], in_recv_sem.at[my_chunk]).start()

    def hold(to_side):
        return tgt_raw.at[pl.ds(2 * to_side, 2)], tgt.at[pl.ds(2 * core, 2)]

    across_source, across_place = hold(1 - side)
    tgt_across = pltpu.make_async_remote_copy(
        src_ref=across_source,
        dst_ref=across_place,
        send_sem=tgt_sem.at[0],
        recv_sem=tgt_sem.at[1],
        device_id=to_seg(spot * 4 + (1 - side) * 2 + side),
        device_id_type=MESH,
    )
    tgt_across.start()
    near_source, near_place = hold(side)
    near_stays = core == side

    @pl.when(near_stays)
    def _():
        pltpu.make_async_copy(near_source, near_place, tgt_sem.at[1]).start()

    @pl.when(jnp.logical_not(near_stays))
    def _():
        pltpu.make_async_remote_copy(
            src_ref=near_source,
            dst_ref=near_place,
            send_sem=tgt_sem.at[2],
            recv_sem=tgt_sem.at[1],
            device_id=to_seg(spot * 4 + side * 3),
            device_id_type=MESH,
        ).start()

    ahead = lax.rem(spot * 2 + side + WORKS - 1, WORKS)
    heads = [
        (tgt_rows.at[pl.ds(2 * to_side, 2), pl.ds(0, 8), :], device_of(ahead, to_side))
        for to_side in range(2)
    ]
    for at, (source, there) in enumerate(heads):

        @pl.when((core == 0) & (there != me))
        def _(at=at, source=source, there=there):
            pltpu.make_async_remote_copy(
                src_ref=source,
                dst_ref=tgt_next,
                send_sem=tgt_sem.at[3 + at],
                recv_sem=tgt_sem.at[5],
                device_id=to_seg(there),
                device_id_type=MESH,
            ).start()

        @pl.when((core == 0) & (there == me))
        def _(source=source):
            pltpu.make_async_copy(source, tgt_next, tgt_sem.at[5]).start()

    row = lax.broadcasted_iota(jnp.int32, (ROWS, 1), 0)
    row_clip = row // 32
    row_hop = lax.rem(row, 32)
    row_length = jnp.where(
        lax.rem(row_clip, 2) == 0, lengths_ref[2 * side], lengths_ref[2 * side + 1]
    )
    inside = work * (2 * HOPS) + (row_clip // 2) * HOPS + row_hop < row_length
    usable = inside & (row_hop < HOPS)
    log_weight = (2.0 * SCALE) / (row_length * BINS).astype(F32)
    for level in range(2):
        mag_windows[level] = jnp.zeros((ROWS, NFFT), F32)

    table_copies[3].wait()
    for turn in range(4):
        chunk = lax.rem(my_chunk + (3 - turn), 4)
        slabs = pl.ds(pl.multiple_of(chunk * SLABS, SLABS), SLABS)
        pltpu.make_async_copy(
            send_in.at[slabs], recv_in.at[slabs], in_recv_sem.at[chunk]
        ).wait()
        arrived = recv_in[slabs].astype(F32).reshape(4, 4, HOPS, 128)
        by_source = [arrived[:, i].reshape(4 * HOPS, 128) for i in range(4)]
        by_clip = swap_lane_groups(by_source)
        for c in range(LOCAL_CLIPS):
            for g in range(4):
                block = by_clip[c][g * HOPS : (g + 1) * HOPS]
                block = jnp.concatenate([block, jnp.zeros((8, 128), F32)], axis=0)
                chunk_in[c * 32 : (c + 1) * 32, g * 128 : (g + 1) * 128] = block.astype(BF16)
        for tile in range(4):
            columns = slice(tile * 512, (tile + 1) * 512)
            product = matmul(
                chunk_in[...], syn[pl.ds(pl.multiple_of(chunk * 512, 512), 512), columns]
            )
            if turn == 0:
                windows[:, columns] = product
            else:
                windows[:, columns] = windows[:, columns] + product

    def neighbours(tail_source, tail, head_source, head, sem):
        return (
            pltpu.make_async_remote_copy(
                src_ref=tail_source,
                dst_ref=tail,
                send_sem=sem.at[0],
                recv_sem=sem.at[1],
                device_id=to_seg(after),
                device_id_type=MESH,
            ),
            pltpu.make_async_remote_copy(
                src_ref=head_source,
                dst_ref=head,
                send_sem=sem.at[2],
                recv_sem=sem.at[3],
                device_id=to_seg(before),
                device_id_type=MESH,
            ),
        )

    def joined(own, tail, head):
        before_us = jnp.where(work == 0, 0.0, tail)
        hop = lax.broadcasted_iota(jnp.int32, head.shape, 1)
        after_us = jnp.where(hop < 3, head, 0.0)
        one, two = own[:2], own[2:]
        spill = one[:, HOPS:]
        middle = jnp.where(hop < 3, spill + two[:, :8], 0.0)
        one = jnp.concatenate([one[:, :8] + before_us, one[:, 8:HOPS], middle], axis=1)
        two = jnp.concatenate(
            [two[:, :8] + spill, two[:, 8:HOPS], two[:, HOPS:] + after_us], axis=1
        )
        whole = jnp.concatenate([one, two], axis=0)
        return jnp.where(inside, whole.reshape(ROWS, HOP), 0.0)

    est_own[...] = overlap_add(windows).reshape(LOCAL_CLIPS, 32, HOP)
    est_copies = neighbours(
        est_own.at[pl.ds(2, 2), pl.ds(HOPS, 8), :],
        est_tail,
        est_own.at[pl.ds(0, 2), pl.ds(0, 8), :],
        est_head,
        est_sem,
    )
    for copy in est_copies:
        copy.start()

    pltpu.make_async_copy(tgt_raw, tgt, tgt_sem.at[1]).wait()
    pltpu.make_async_copy(tgt_next, tgt_next, tgt_sem.at[5]).wait()
    own = tgt[...].astype(F32)
    first_half = jnp.concatenate([own[:2], own[2:, :8]], axis=1)
    second_half = jnp.concatenate([own[2:], tgt_next[...]], axis=1)
    own = jnp.concatenate([first_half, second_half], axis=0).reshape(ROWS, HOP)
    write_windows(tgt_win, jnp.where(inside, own, 0.0))

    def frames_of(windows_ref, points):
        stride = points // 4
        parts = [
            windows_ref[:, at * stride : at * stride + points] for at in range(HOP // stride)
        ]
        return parts[0] if len(parts) == 1 else jnp.concatenate(parts, axis=0)

    for level, points in enumerate(SIZES):
        half = points // 2
        count = NFFT // points
        table_copies[level].wait()

        def target_columns(step, energy, level=level, points=points, half=half, count=count):
            column = pl.multiple_of(step * 256, 256)
            frames = frames_of(tgt_win, points)
            real = matmul(frames, analysis[level][:, pl.ds(column, 256)])
            imag = matmul(frames, analysis[level][:, pl.ds(half + column, 256)])
            power = real * real + imag * imag + EPS_MAG
            for at in range(count):
                place = pl.ds(pl.multiple_of(at * half + column, 256), 256)
                part = power[at * ROWS : (at + 1) * ROWS]
                tgt_mag[level, :, place] = jnp.sqrt(part)
                tgt_log[level, :, place] = 0.5 * jnp.log(part)
                energy = energy + fold_rows(jnp.where(usable, part, 0.0))
            return energy

        start = jnp.zeros((LOCAL_CLIPS, 8, 128), F32)
        sums[3 + level] = lax.fori_loop(0, half // 256, target_columns, start, unroll=True)

    for copy in est_copies:
        copy.wait_recv()
    write_windows(est_win, joined(est_own[...], est_tail[...], est_head[...]))

    for level, points in enumerate(SIZES):
        half = points // 2
        count = NFFT // points
        spread = jnp.zeros((LOCAL_CLIPS, 8, 128), F32)
        logterm = jnp.zeros((LOCAL_CLIPS, 8, 128), F32)
        for column in range(0, half, 256):
            frames = frames_of(est_win, points)
            all_real = matmul(frames, analysis[level][:, column : column + 256])
            all_imag = matmul(frames, analysis[level][:, half + column : half + column + 256])
            for at in range(count):
                rows = slice(at * ROWS, (at + 1) * ROWS)
                real, imag = all_real[rows], all_imag[rows]
                power = real * real + imag * imag + EPS_MAG
                inverse = lax.rsqrt(power)
                place = slice(at * half + column, at * half + column + 256)
                gap = power * inverse - tgt_mag[level, :, place]
                log_gap = 0.5 * jnp.log(power) - tgt_log[level, :, place]
                mag_factor = jnp.where(usable, gap * inverse, 0.0)
                log_factor = jnp.where(usable, log_gap * inverse * inverse * log_weight, 0.0)
                for part, first in (
                    (real, at * points + column),
                    (imag, at * points + half + column),
                ):
                    lanes = slice(first, first + 256)
                    grad_x[level, :ROWS, lanes] = (mag_factor * part).astype(BF16)
                    grad_x[level, ROWS:, lanes] = (log_factor * part).astype(BF16)
                spread = spread + fold_rows(jnp.where(usable, gap * gap, 0.0))
                logterm = logterm + fold_rows(jnp.where(usable, log_gap * log_gap, 0.0))
        sums[level] = spread
        sums[6 + level] = logterm

    flat = sums[...].reshape(36, 8, 128).sum(axis=1)
    flat = jnp.sum(flat, axis=1, keepdims=True)
    lane = lax.broadcasted_iota(jnp.int32, (36, 128), 1)
    line = lax.broadcasted_iota(jnp.int32, (36, 128), 0)
    own_stats = jnp.sum(jnp.where(lane == line, flat, 0.0), axis=0, keepdims=True)
    stat_send[...] = own_stats
    stat_recv[work] = own_stats

    def send_stats(step, carry):
        pltpu.make_async_remote_copy(
            src_ref=stat_send,
            dst_ref=stat_recv.at[work],
            send_sem=stat_sem.at[0],
            recv_sem=stat_sem.at[1],
            device_id=to_seg(device_of(lax.rem(work + step, WORKS), side)),
            device_id_type=MESH,
        ).start()
        return carry

    lax.fori_loop(1, WORKS, send_stats, 0)
    def add_to(ref, first, product):
        ref[:, first : first + 256] = ref[:, first : first + 256] + product

    for step in range(0, NFFT, 256):
        product = matmul_nt(grad_x[2], a2048[step : step + 256, :])
        mag_windows[2, :, step : step + 256] = product[:ROWS]
        windows[:, step : step + 256] = product[ROWS:]
    for level, points in ((1, 1024), (0, 512)):
        count = NFFT // points
        stacked = jnp.concatenate(
            [grad_x[level, :, at * points : (at + 1) * points] for at in range(count)], axis=0
        )
        for step in range(0, points, 256):
            product = matmul_nt(stacked, analysis[level][step : step + 256, :])
            for at in range(count):
                first = at * (points // 4) + step
                base = at * 2 * ROWS
                add_to(mag_windows.at[level], first, product[base : base + ROWS])
                add_to(windows, first, product[base + ROWS : base + 2 * ROWS])

    for level in range(3):
        grad_own[level] = overlap_add(mag_windows.at[level], level + 2)
    grad_own[3] = overlap_add(windows)
    hop8 = lax.broadcasted_iota(jnp.int32, (2, 8, HOP), 1)
    for pair in range(2):
        upper = grad_own[2 * pair].reshape(LOCAL_CLIPS, 32, HOP)
        lower = grad_own[2 * pair + 1].reshape(LOCAL_CLIPS, 32, HOP)
        tail_send[pair] = jnp.where(
            hop8 < 4, upper[2:, HOPS:], pltpu.roll(lower[2:, HOPS:], 4, 1)
        )
        head_send[pair] = jnp.where(hop8 < 4, upper[:2, :8], pltpu.roll(lower[:2, :8], 4, 1))
    grad_copies = neighbours(tail_send, grad_tail, head_send, grad_head, grad_sem)
    for copy in grad_copies:
        copy.start()

    others = stat_recv.at[pl.ds(0, WORKS - 1)]
    pltpu.make_async_copy(others, others, stat_sem.at[1]).wait()
    totals = stat_recv[...].sum(axis=0)

    place = lax.broadcasted_iota(jnp.int32, (1, 128), 1)
    low_half = lax.rem(place, 4) < 2
    totals = totals + jnp.where(low_half, pltpu.roll(totals, 126, 1), pltpu.roll(totals, 2, 1))
    energy = pltpu.roll(totals, 128 - 12, 1)
    logterm = pltpu.roll(totals, 128 - 24, 1)
    filled = place < 12
    lane_length = jnp.where(
        lax.rem(place, 2) == 0, lengths_ref[2 * side], lengths_ref[2 * side + 1]
    )
    entries = (lane_length * BINS).astype(F32)
    safe_energy = jnp.where(filled, energy, 1.0)
    safe_spread = jnp.where(filled, totals, 1.0) + EPS_RATIO
    terms = jnp.where(filled & low_half, jnp.sqrt(safe_spread / safe_energy) + logterm / entries, 0.0)
    weights = SCALE / jnp.sqrt(safe_spread * safe_energy)
    weights = jnp.broadcast_to(weights, (ROWS, 128))
    pick_lane = lax.broadcasted_iota(jnp.int32, (ROWS, 128), 1)
    pick_row = lax.broadcasted_iota(jnp.int32, (ROWS, 128), 0) // 32
    mag_weights = [
        jnp.sum(jnp.where(pick_lane == level * 4 + pick_row, weights, 0.0), axis=1, keepdims=True)
        for level in range(3)
    ]
    own = grad_own[3]
    for level in range(3):
        own = own + mag_weights[level] * grad_own[level]
    for copy in grad_copies:
        copy.wait_recv()

    def weighted(received):
        def row_of(component):
            block = received[component // 2]
            return block if component % 2 == 0 else pltpu.roll(block, 4, 1)

        total = row_of(3)
        for level in range(3):
            weight = mag_weights[level].reshape(LOCAL_CLIPS, 32, 1)[:2, :8]
            total = total + weight * row_of(level)
        return jnp.where(hop8 < 3, total, 0.0)

    write_windows(
        grad_win,
        joined(own.reshape(LOCAL_CLIPS, 32, HOP), weighted(grad_tail), weighted(grad_head)),
    )

    first_tile = me // 8 + 1

    def back_bins(step, carry):
        tile = lax.rem(first_tile + step, 8)
        product = matmul_nt(grad_win[...], syn[pl.ds(pl.multiple_of(tile * 256, 256), 256), :])
        for g in range(2):
            lanes = product[:, g * 128 : (g + 1) * 128]
            by_clip = [lanes[c * 32 : c * 32 + HOPS] for c in range(LOCAL_CLIPS)]
            for i, block in enumerate(swap_lane_groups(by_clip)):
                send_out[tile * 8 + g * 4 + i] = block.astype(BF16)
        for i in range(8):
            there = tile * 8 + i

            @pl.when(there != me)
            def _():
                pltpu.make_async_remote_copy(
                    src_ref=send_out.at[there],
                    dst_ref=recv_out.at[my_slot],
                    send_sem=out_send_sem,
                    recv_sem=out_recv_sem.at[my_chunk],
                    device_id=to_seg(there),
                    device_id_type=MESH,
                ).start()

            @pl.when(there == me)
            def _():
                pltpu.make_async_copy(
                    send_out.at[me], recv_out.at[my_slot], out_recv_sem.at[my_chunk]
                ).start()

        return carry

    lax.fori_loop(0, 8, back_bins, 0)

    own_loss = jnp.sum(terms, axis=1, keepdims=True) + jnp.zeros((1, 128), F32)
    loss_send[...] = own_loss
    my_loss = clip * 2 + side
    loss_recv[my_loss] = own_loss
    for peer in loss_peers:
        pltpu.make_async_remote_copy(
            src_ref=loss_send,
            dst_ref=loss_recv.at[my_loss],
            send_sem=loss_sem.at[0],
            recv_sem=loss_sem.at[1],
            device_id=peer,
            device_id_type=MESH,
        ).start()

    seven = loss_recv.at[pl.ds(0, 2 * CLIP_GROUPS - 1)]
    pltpu.make_async_copy(seven, seven, loss_sem.at[1]).wait()
    loss_ref[...] = loss_recv[...].sum(axis=0) / (3 * CLIPS)

    for turn in range(4):
        chunk = lax.rem(my_chunk + (3 - turn), 4)
        slabs = pl.ds(pl.multiple_of(chunk * SLABS, SLABS), SLABS)
        pltpu.make_async_copy(
            send_out.at[slabs], recv_out.at[slabs], out_recv_sem.at[chunk]
        ).wait()
        arrived = recv_out[slabs].astype(F32)
        one, two = halves(arrived[:8], arrived[8:])
        whole = jnp.concatenate([one[:, None], two[:, None]], axis=1)
        turned = whole.reshape(SLABS * HOPS, 128).T
        out_ref[:, pl.ds(pl.multiple_of(chunk * 384, 128), 384)] = turned.astype(BF16)

    for copy in est_copies + grad_copies + (tgt_across,):
        copy.wait_send()

    @pl.when(jnp.logical_not(near_stays))
    def _():
        pltpu.make_async_copy(near_source, near_source, tgt_sem.at[2]).wait()

    for at, (source, there) in enumerate(heads):

        @pl.when((core == 0) & (there != me))
        def _(at=at):
            pltpu.make_async_copy(tgt_next, tgt_next, tgt_sem.at[3 + at]).wait()

    pltpu.make_async_copy(others, others, stat_sem.at[0]).wait()
    pltpu.make_async_copy(seven, seven, loss_sem.at[0]).wait()
    sent = pl.ds(0, SEGS - 1)
    pltpu.make_async_copy(send_in.at[sent], recv_in.at[sent], in_send_sem).wait()
    pltpu.make_async_copy(send_out.at[sent], recv_out.at[sent], out_send_sem).wait()


def body(spectra, target, lengths):
    vmem = pl.BlockSpec(memory_space=pltpu.VMEM)
    smem = pl.BlockSpec(memory_space=pltpu.SMEM)
    anywhere = pl.BlockSpec(memory_space=pl.ANY)
    slabs = pltpu.VMEM((SEGS, HOPS, 128), BF16)
    pairs = pltpu.VMEM((2, 2, 8, HOP), F32)
    hops8 = pltpu.VMEM((2, 8, HOP), F32)
    hops24 = pltpu.VMEM((LOCAL_CLIPS, HOPS, HOP), BF16)
    hops32 = pltpu.VMEM((LOCAL_CLIPS, 32, HOP), F32)
    window = pltpu.VMEM((ROWS, NFFT), BF16)
    entries = pltpu.VMEM((3, ROWS, BINS), F32)
    dma = pltpu.SemaphoreType.DMA
    out, loss = pl.pallas_call(
        kernel,
        out_shape=(
            jax.ShapeDtypeStruct((ROWS, FRAMES), BF16),
            jax.ShapeDtypeStruct((1, 128), F32),
        ),
        in_specs=[vmem, vmem, smem] + [anywhere] * 4,
        out_specs=(vmem, vmem),
        scratch_shapes=[
            slabs, slabs, pltpu.VMEM((ROWS, 512), BF16), slabs, slabs,
            pltpu.VMEM((LOCAL_CLIPS, HOPS, HOP), F32), hops24, hops8,
            pltpu.VMEM((2048, 2048), BF16), pltpu.VMEM((512, 512), BF16),
            pltpu.VMEM((1024, 1024), BF16), pltpu.VMEM((2048, 2048), BF16),
            hops24, window, hops32, hops8, hops8, window,
            pltpu.VMEM((ROWS, NFFT), F32), pltpu.VMEM((3, ROWS, NFFT), F32), entries, entries,
            pltpu.VMEM((3, 2 * ROWS, NFFT), BF16),
            pltpu.VMEM((4, ROWS, HOP), F32), pairs, pairs, pairs, pairs, window,
            pltpu.VMEM((9, LOCAL_CLIPS, 8, 128), F32),
            pltpu.VMEM((1, 128), F32), pltpu.VMEM((WORKS, 1, 128), F32),
            pltpu.VMEM((1, 128), F32), pltpu.VMEM((2 * CLIP_GROUPS, 1, 128), F32),
            dma((4,)), dma, dma((4,)), dma, dma((4,)),
            dma((6,)), dma((4,)), dma((4,)), dma((2,)), dma((2,)),
        ],
        compiler_params=pltpu.CompilerParams(
            collective_id=0, has_side_effects=True, vmem_limit_bytes=60 * 2**20
        ),
        cost_estimate=pl.CostEstimate(
            flops=8 * 10**9, bytes_accessed=20 * 10**6, transcendentals=10**6
        ),
    )(
        spectra.reshape(ROWS, FRAMES),
        target,
        lengths,
        jnp.asarray(synthesis_table()),
        *(jnp.asarray(analysis_table(points)) for points in SIZES),
    )
    return loss[0, 0], out.reshape(LOCAL_CLIPS, 2, BINS // SEGS, FRAMES)


def solution(mesh):
    placed = (P("clip", None, "seg", None), P("clip", "seg"), P("clip"))
    return jax.shard_map(
        body,
        mesh=mesh,
        in_specs=placed,
        out_specs=(P(), P("clip", None, "seg", None)),
        check_vma=False,
    )
```
